256 devices in a mesh: segment: 4 (over x), dom: 64 (over z, y, core).
Axes of the slice: x: 4, y: 4, z: 8, core: 2. Of those that a mesh axis runs over, the one named last changes fastest.
Arguments:
- samples: bfloat16 [4, 32768, 512], P(None, 'dom'), may hold values from -6 to 6
- w_source: bfloat16 [4, 1, 512, 512], P('segment'), may hold values from -0.25 to 0.25
- w_self: bfloat16 [4, 1, 512, 512], P('segment'), may hold values from -0.25 to 0.25
- w_message: bfloat16 [4, 1, 512, 512], P('segment'), may hold values from -0.25 to 0.25
- w_output: bfloat16 [4, 1, 512, 512], P('segment'), may hold values from -0.25 to 0.25
- norm_gain: float32 [4, 1, 512], P('segment'), may hold values from 0.1 to 1.9
- tile_source: int32 [4, 256, 6], P('segment', 'dom'), may hold values from 0 to 255, as said below
- tile_count: int32 [4, 256], P('segment', 'dom'), may hold values from 3 to 6, as said below
- tile_value: bfloat16 [4, 256, 6, 128, 128], P('segment', 'dom'), may hold values from -0.21875 to 0.21875
Outputs:
- final: bfloat16 [4, 32768, 512], P('segment', 'dom')
The draws below stay inside these ranges and needn't reach their ends.
Inputs may be any that keep to these rules, and one draw needn't show every extreme that they name: `tile_source`: each entry for destination block b names a block among the 4 blocks that hold b's dom index (blocks (b // 4) * 4 .. + 4 - 1) or the 1 block on either side of them, counted cyclically over 256. `tile_count`: slots at or beyond the count are unused; the first block of every dom index uses all 6 slots.
All inputs are finite; a program needn't handle non-finite values.
Results may differ from the reference program's by a relative error of at most 0.013.
Values may be sent and summed in bfloat16 or wider, within the bound.
No kernel may reach another device: no remote copies, remote signals or barrier semaphores. Data moves between devices by JAX's collectives and lax.ppermute only.
A program may use at most 64 MiB of HBM per device.

```python
import jax
import jax.numpy as jnp
from jax import lax

D = 512
BLK = 128
BD = 4
HB = 1
K = 6
LPS = 1
SAMPLES = 4
SEGMENTS = 4
NBLK = 256
NODES = 32768


def draw_tile_source(key, part):
    blocks = jnp.arange(NBLK, dtype=jnp.int32)
    base = blocks // BD * BD - HB
    offsets = jax.random.randint(jax.random.fold_in(key, 11), (SEGMENTS, NBLK, K), 0, BD + 2 * HB)
    lower = jax.random.randint(jax.random.fold_in(key, 12), (SEGMENTS, NBLK), 0, HB)
    upper = jax.random.randint(jax.random.fold_in(key, 13), (SEGMENTS, NBLK), BD + HB, BD + 2 * HB)
    own = jnp.broadcast_to(blocks % BD + HB, (SEGMENTS, NBLK))
    offsets = offsets.at[:, :, 0].set(own)
    offsets = offsets.at[:, :, 1].set(lower)
    offsets = offsets.at[:, :, 2].set(upper)
    return jnp.mod(base[None, :, None] + offsets, NBLK).astype(jnp.int32)


def draw_tile_count(key, part):
    counts = jax.random.randint(jax.random.fold_in(key, 21), (SEGMENTS, NBLK), 3, K + 1)
    first = (jnp.arange(NBLK, dtype=jnp.int32) % BD == 0)[None, :]
    return jnp.where(first, K, counts).astype(jnp.int32)


def steps_of(key, dims, shards, low, largest):
    def one(axis_at, shards_of):
        steps = jax.random.uniform(jax.random.fold_in(jax.random.fold_in(key, 6), axis_at), (shards_of,), jnp.float32, low / len(shards), largest / len(shards))
        return jnp.repeat(jnp.exp(steps), dims[axis_at] // shards_of).reshape((-1,) + (1,) * (len(dims) - axis_at - 1))

    gain = one(*shards[0])
    for cut in shards[1:]:
        gain = gain * one(*cut)
    return gain


def noise(stream_key, dims, width, limit, split=(), kind=jnp.bfloat16):
    entries = jax.random.normal(stream_key, dims, jnp.float32) * width
    if len(split) > 0:
        entries = steps_of(stream_key, dims, split, -0.22, 0.18) * entries
    return jnp.clip(entries, min=-limit, max=limit).astype(kind)


def setup_inputs(seed: int = 0) -> dict:
    arg_keys = jax.random.split(jax.random.key(seed), 10)
    samples = noise(arg_keys[0], (SAMPLES, NODES, D), 1.0, 6.0, ((1, 64),))
    w_source = noise(arg_keys[1], (SEGMENTS, LPS, D, D), D ** -0.5, 0.25, ((0, 4),))
    w_self = noise(arg_keys[2], (SEGMENTS, LPS, D, D), D ** -0.5, 0.25, ((0, 4),))
    w_message = noise(arg_keys[3], (SEGMENTS, LPS, D, D), D ** -0.5, 0.25, ((0, 4),))
    w_output = noise(arg_keys[4], (SEGMENTS, LPS, D, D), D ** -0.5, 0.25, ((0, 4),))
    norm_gain = jnp.clip(1.0 + 0.18 * jax.random.normal(arg_keys[5], (SEGMENTS, LPS, D), jnp.float32), 0.1, 1.9)
    tile_source = draw_tile_source(jax.random.fold_in(arg_keys[9], 71), 0)
    tile_count = draw_tile_count(jax.random.fold_in(arg_keys[9], 71), 0)
    tile_value = noise(arg_keys[8], (SEGMENTS, NBLK, K, BLK, BLK), (BLK * K) ** -0.5, 0.21875, ((0, 4), (1, 64)))
    return dict(samples=samples, w_source=w_source, w_self=w_self, w_message=w_message, w_output=w_output, norm_gain=norm_gain, tile_source=tile_source, tile_count=tile_count, tile_value=tile_value)


def run_layer(h, w_source, w_self, w_message, w_output, norm_gain, sources, counts, tiles):
    sender = jax.nn.silu(jnp.dot(h, w_source, preferred_element_type=jnp.float32)).astype(jnp.bfloat16)
    sender_blocks = sender.reshape(NBLK, BLK, D)
    slots = jnp.arange(K, dtype=jnp.int32)

    def one_block(packed):
        src_row, count_one, tile_set = packed
        keep = (slots < count_one).astype(jnp.float32)
        weights = tile_set.astype(jnp.float32) * keep[:, None, None]
        picked = sender_blocks[src_row.astype(jnp.int32)].astype(jnp.float32)
        return jnp.einsum('kij,kjd->id', weights, picked)
    gathered = lax.map(one_block, (sources, counts, tiles)).reshape(NODES, D).astype(jnp.bfloat16)
    mixed = jnp.dot(h, w_self, preferred_element_type=jnp.float32) + jnp.dot(gathered, w_message, preferred_element_type=jnp.float32)
    scaled = mixed / jnp.sqrt(lax.optimization_barrier(jnp.mean(mixed * mixed, axis=-1, keepdims=True)) + 1e-05) * norm_gain
    update = jax.nn.silu(scaled).astype(jnp.bfloat16)
    return (h.astype(jnp.float32) + jnp.dot(update, w_output, preferred_element_type=jnp.float32)).astype(jnp.bfloat16)

def reference(samples, w_source, w_self, w_message, w_output, norm_gain, tile_source, tile_count, tile_value):
    outputs = []
    for sample in range(SAMPLES):
        h = samples[sample]
        for section in range(SEGMENTS):
            for layer in range(LPS):
                h = run_layer(h, w_source[section, layer], w_self[section, layer], w_message[section, layer], w_output[section, layer], norm_gain[section, layer], tile_source[section], tile_count[section], tile_value[section])
        outputs.append(h)
    return jnp.stack(outputs)
```

```python
import functools

import jax
import jax.numpy as jnp
from jax import lax
from jax.experimental import pallas as pl
from jax.experimental.pallas import tpu as pltpu
from jax.sharding import PartitionSpec as P

D = 512
BLK = 128
BD = 4
K = 6
SEG = 4
Y, Z = 4, 8
HALF = D // 2
META = 16
BF = jnp.bfloat16
F32 = jnp.float32
ANY = pl.BlockSpec(memory_space=pl.ANY)
SMEM = pl.BlockSpec(memory_space=pltpu.SMEM)
VMEM = pl.BlockSpec(memory_space=pltpu.VMEM)


def silu(v):
    return (0.5 * v) * (1.0 + jnp.tanh(0.5 * v))


def params(mib):
    return pltpu.CompilerParams(vmem_limit_bytes=mib * 2**20)


def by_segment(x):
    return [(i, i ^ x) for i in range(SEG)]


def shifted(by):
    return [(i, (i + by) % SEG) for i in range(SEG)]


def dom_pairs(move):
    out = []
    for d in range(Z * Y * 2):
        z, y, c = move(d // (2 * Y), d // 2 % Y, d % 2)
        out.append((d, ((z % Z) * Y + y % Y) * 2 + c % 2))
    return out


def along_y(by):
    return dom_pairs(lambda z, y, c: (z, y + by, c))


def along_z(by):
    return dom_pairs(lambda z, y, c: (z + by, y, c))


def to_dom(by):
    n = Z * Y * 2
    return [(i, (i + by) % n) for i in range(n)]


OTHER_CORE = dom_pairs(lambda z, y, c: (z, y, c + 1))


def pack_kernel(scal, src, cnt, gain, w0, w1, w2, w3, out, buf, sem):
    y, zpar, c, dom = scal[1], scal[2], scal[3], scal[8]
    for m, w in enumerate((w0, w1, w2, w3)):

        @pl.when(y == m)
        def _():
            pltpu.make_async_copy(
                w.at[
                    0,
                    0,
                    pl.ds(pl.multiple_of(zpar * HALF, HALF), HALF),
                    pl.ds(pl.multiple_of(c * HALF, HALF), HALF),
                ],
                buf,
                sem,
            ).start()

    row = lax.broadcasted_iota(jnp.int32, (META, HALF), 0)
    col = lax.broadcasted_iota(jnp.int32, (META, HALF), 1)
    meta = jnp.zeros((META, HALF), F32)
    for b in range(BD):
        for k in range(K):
            rel = (src[0, b, k] - (dom * BD - 1) + 512) & 255
            code = jnp.where(k < cnt[0, b], rel, 7).astype(F32)
            meta = jnp.where((row == 0) & (col == b * K + k), code, meta)
    left = gain[0]
    for part in range(3):
        piece = left.astype(BF).astype(F32)
        left = left - piece
        for half in range(2):
            meta = jnp.where(
                row == 2 + 2 * part + half, piece[:, half * HALF : (half + 1) * HALF], meta
            )
    out[HALF:, :] = meta.astype(BF)
    pltpu.make_async_copy(out.at[:HALF], buf, sem).wait()
    out[:HALF, :] = buf[...]


def pack(scal, src, cnt, gain, ws):
    return pl.pallas_call(
        pack_kernel,
        out_shape=jax.ShapeDtypeStruct((HALF + META, HALF), BF),
        in_specs=[SMEM, SMEM, SMEM, VMEM] + [ANY] * 4,
        out_specs=VMEM,
        scratch_shapes=[pltpu.VMEM((HALF, HALF), BF), pltpu.SemaphoreType.DMA],
        compiler_params=params(4),
        name="pack",
    )(scal, src, cnt, gain, *ws)


def start_weights(scal, section, own, stages, mats, wbuf, wsem):
    p, zpar, c = scal[0], scal[2], scal[3]

    @pl.when(p == section)
    def _():
        for i, m in enumerate(mats):
            pltpu.make_async_copy(own[i].at[0, 0], wbuf.at[i], wsem.at[i]).start()

    by_stage = {}
    for q in range(SEG):
        if q != section:
            by_stage.setdefault(section - (1 if section > q else 0), []).append(q)
    for j, holders in by_stage.items():
        cond = functools.reduce(jnp.logical_or, [p == q for q in holders])

        @pl.when(cond)
        def _():
            for i, m in enumerate(mats):
                r = scal[4 + m]
                for core in range(2):
                    for zrel in range(2):
                        rows = pl.multiple_of(((zpar + zrel) & 1) * HALF, HALF)
                        cols = pl.multiple_of(((c + core) & 1) * HALF, HALF)
                        pltpu.make_async_copy(
                            stages[j][core].at[zrel * 4 + r],
                            wbuf.at[i, pl.ds(rows, HALF), pl.ds(cols, HALF)],
                            wsem.at[i],
                        ).start()


def wait_weight(own, i, wbuf, wsem):
    pltpu.make_async_copy(own[i].at[0, 0], wbuf.at[i], wsem.at[i]).wait()


def tile_halves(section, p):
    k = (p - section) % SEG
    if k == 0:
        return "ownA", "ownB"
    if k == 1:
        return "r1p", ("r2p" if p == 1 else "r3p")
    if k == 2:
        return ("r3p" if p == 1 else "r2p"), ("r3m" if p == 3 else "r2m")
    return ("r2m" if p == 3 else "r3m"), "r1m"


def start_tiles(scal, section, own, moved, tbuf, tsem):
    for q in range(SEG):

        @pl.when(scal[0] == q)
        def _():
            for half, name in enumerate(tile_halves(section, q)):
                src = own.at[0, pl.ds(2 * half, 2)] if name.startswith("own") else moved[name]
                pltpu.make_async_copy(src, tbuf.at[pl.ds(2 * half, 2)], tsem.at[half]).start()


def section_kernel(section, names, n_stage, scal, ints, meta, h, below, above, *rest):
    first = section == 0
    mats = (0, 1, 2, 3) if first else (1, 2, 3)
    n = len(mats)
    rest = list(rest)
    if not first:
        sender = rest.pop(0)
    own, rest = rest[:n], rest[n:]
    stages, rest = [rest[2 * j : 2 * j + 2] for j in range(n_stage)], rest[2 * n_stage :]
    tiles = rest.pop(0)
    moved = dict(zip(names, rest))
    rest = rest[len(names) :]
    out, wbuf, tbuf, sbuf, gbuf, hbuf, wsem, tsem, hsem = rest

    start_weights(scal, section, own, stages, mats, wbuf, wsem)
    if first:
        pltpu.make_async_copy(h.at[scal[0]], hbuf, hsem).start()
    else:
        pltpu.make_async_copy(h, hbuf, hsem).start()
    start_tiles(scal, section, tiles, moved, tbuf, tsem)
    x = scal[0] ^ section
    if first:
        pltpu.make_async_copy(h.at[0], hbuf, hsem).wait()
        wait_weight(own, 0, wbuf, wsem)
        w = wbuf[0]
        for rows, src in ((0, below), (5 * BLK, above)):
            s = silu(jnp.dot(src[...], w, preferred_element_type=F32)).astype(BF)
            sbuf[rows : rows + BLK, :] = s
        for i in range(2):
            s = jnp.dot(hbuf[i * HALF : (i + 1) * HALF, :], w, preferred_element_type=F32)
            sbuf[BLK + i * HALF : BLK + (i + 1) * HALF, :] = silu(s).astype(BF)
    else:
        sbuf[:BLK, :] = below[...]
        sbuf[BLK : 5 * BLK, :] = sender[...]
        sbuf[5 * BLK :, :] = above[...]
        pltpu.make_async_copy(h, hbuf, hsem).wait()
    for half in range(2):
        pltpu.make_async_copy(
            tiles.at[0, pl.ds(2 * half, 2)], tbuf.at[pl.ds(2 * half, 2)], tsem.at[half]
        ).wait()
    for b in range(BD):
        left, right = [], []
        for k in range(K):
            code = ints[x, b * K + k]
            used = code < 7
            at = pl.multiple_of(jnp.where(used, code, 0) * BLK, BLK)
            tile = tbuf[b, k]
            left.append(jnp.where(used, tile, jnp.zeros_like(tile)))
            right.append(sbuf[pl.ds(at, BLK), :])
        got = jnp.dot(
            jnp.concatenate(left, axis=1),
            jnp.concatenate(right, axis=0),
            preferred_element_type=F32,
        )
        gbuf[b * BLK : (b + 1) * BLK, :] = got.astype(BF)
    for i in range(n - 3, n):
        wait_weight(own, i, wbuf, wsem)
    m = meta[x].astype(F32)
    gain = jnp.concatenate(
        [m[2 + h : 3 + h, :] + (m[4 + h : 5 + h, :] + m[6 + h : 7 + h, :]) for h in range(2)],
        axis=1,
    )
    for i in range(2):
        rows = slice(i * HALF, (i + 1) * HALF)
        mixed = jnp.dot(hbuf[rows, :], wbuf[n - 3], preferred_element_type=F32)
        mixed = mixed + jnp.dot(gbuf[rows, :], wbuf[n - 2], preferred_element_type=F32)
        mean = jnp.mean(mixed * mixed, axis=-1, keepdims=True)
        scaled = mixed * lax.rsqrt(mean + 1e-05) * gain
        update = silu(scaled).astype(BF)
        new = hbuf[rows, :].astype(F32) + jnp.dot(
            update, wbuf[n - 1], preferred_element_type=F32
        )
        out[rows, :] = new.astype(BF)


def section_call(section, scal, ints, meta, h, below, above, sender, own, stages, tiles, moved):
    first = section == 0
    mats = (0, 1, 2, 3) if first else (1, 2, 3)
    own = [own[m] for m in mats]
    flat = [a for pair in stages for a in pair]
    args = [scal, ints, meta, h, below, above]
    specs = [SMEM, SMEM, VMEM, ANY, VMEM, VMEM]
    if not first:
        args.append(sender)
        specs.append(VMEM)
    args += own + flat + [tiles] + list(moved.values())
    specs += [ANY] * (len(args) - len(specs))
    n = len(mats)
    return pl.pallas_call(
        functools.partial(section_kernel, section, list(moved), len(stages)),
        out_shape=jax.ShapeDtypeStruct((BD * BLK, D), BF),
        in_specs=specs,
        out_specs=VMEM,
        scratch_shapes=[
            pltpu.VMEM((n, D, D), BF),
            pltpu.VMEM((BD, K, BLK, BLK), BF),
            pltpu.VMEM(((BD + 2) * BLK, D), BF),
            pltpu.VMEM((BD * BLK, D), BF),
            pltpu.VMEM((BD * BLK, D), BF),
            pltpu.SemaphoreType.DMA((4,)),
            pltpu.SemaphoreType.DMA((2,)),
            pltpu.SemaphoreType.DMA,
        ],
        compiler_params=params(24),
        cost_estimate=pl.CostEstimate(
            flops=1_500_000_000, bytes_accessed=4_000_000, transcendentals=262144
        ),
        name=f"section{section}",
    )(*args)


def sender_kernel(section, n_stage, scal, h, own, *rest):
    stages = [rest[2 * j : 2 * j + 2] for j in range(n_stage)]
    full, head, tail, wbuf, wsem = rest[2 * n_stage :]
    start_weights(scal, section, [own], stages, (0,), wbuf, wsem)
    wait_weight([own], 0, wbuf, wsem)
    w = wbuf[0]
    for i in range(2):
        rows = slice(i * HALF, (i + 1) * HALF)
        s = silu(jnp.dot(h[rows, :], w, preferred_element_type=F32)).astype(BF)
        full[rows, :] = s
        if i == 0:
            head[...] = s[:BLK, :]
        else:
            tail[...] = s[HALF - BLK :, :]


def sender_call(section, scal, h, own, stages):
    flat = [a for pair in stages for a in pair]
    return pl.pallas_call(
        functools.partial(sender_kernel, section, len(stages)),
        out_shape=[
            jax.ShapeDtypeStruct((BD * BLK, D), BF),
            jax.ShapeDtypeStruct((BLK, D), BF),
            jax.ShapeDtypeStruct((BLK, D), BF),
        ],
        in_specs=[SMEM, VMEM, ANY] + [ANY] * len(flat),
        out_specs=[VMEM] * 3,
        scratch_shapes=[pltpu.VMEM((1, D, D), BF), pltpu.SemaphoreType.DMA((1,))],
        compiler_params=params(8),
        cost_estimate=pl.CostEstimate(
            flops=270_000_000, bytes_accessed=1_500_000, transcendentals=262144
        ),
        name=f"sender{section}",
    )(scal, h, own, *flat)


def gather_stage(pieces):
    n = pieces.shape[0]
    ring = [pieces] + [lax.ppermute(pieces, "dom", along_y(by)) for by in (1, -1, 2)]
    mine = jnp.stack(ring, axis=1)
    upper = lax.ppermute(mine[:, :, :BLK, :], "dom", along_z(1))
    lower = lax.ppermute(mine[:, :, BLK:, :], "dom", along_z(-1))
    mine = jnp.concatenate([mine, jnp.concatenate([upper, lower], axis=2)], axis=1)
    other = lax.ppermute(mine, "dom", OTHER_CORE)
    return [(mine[i], other[i]) for i in range(n)]


def shards(samples, w_source, w_self, w_message, w_output, norm_gain, tile_source, tile_count, tile_value):
    p = lax.axis_index("segment")
    dom = lax.axis_index("dom")
    c, y, zpar = dom % 2, dom // 2 % Y, dom // (2 * Y) % 2
    steps = jnp.array([0, 2, 3, 1], jnp.int32)
    scal = jnp.stack(
        [p, y, zpar, c] + [steps[(m - y) % Y] for m in range(4)] + [dom]
    ).astype(jnp.int32)
    ws = [w_source, w_self, w_message, w_output]
    packed = pack(scal, tile_source, tile_count, norm_gain, ws)
    crossed = [packed] + [lax.ppermute(packed, "segment", by_segment(x)) for x in (1, 2, 3)]

    h = lax.dynamic_index_in_dim(samples, p, 0, keepdims=False)
    below = lax.ppermute(h[(BD - 1) * BLK :], "dom", to_dom(1))
    above = lax.ppermute(h[:BLK], "dom", to_dom(-1))

    half_a, half_b = tile_value[0, :2], tile_value[0, 2:]
    root = p == 0
    moved = {}
    moved["r1p"] = lax.ppermute(half_a, "segment", shifted(1))
    moved["r1m"] = lax.ppermute(half_b, "segment", shifted(-1))
    moved["r2p"] = lax.ppermute(jnp.where(root, half_b, moved["r1p"]), "segment", shifted(1))
    moved["r2m"] = lax.ppermute(jnp.where(root, half_a, moved["r1m"]), "segment", shifted(-1))
    early = dict(moved)
    moved["r3p"] = lax.ppermute(jnp.where(root, moved["r1p"], half_b), "segment", shifted(1))
    moved["r3m"] = lax.ppermute(jnp.where(root, moved["r1m"], half_a), "segment", shifted(-1))

    meta = jnp.stack([a[HALF:] for a in crossed])
    ints = meta[:, 0, :BLK].astype(jnp.int32)
    need = jnp.array([[1, 2, 3], [1, 3, 2], [2, 3, 1], [3, 2, 1]], jnp.int32)[p]
    parts = jnp.stack([a[:HALF] for a in crossed[1:]])
    stage = [lax.dynamic_index_in_dim(parts, need[j] - 1, 0, keepdims=True) for j in range(3)]
    stages = gather_stage(stage[0])
    stages += gather_stage(jnp.concatenate(stage[1:], axis=0))

    h = section_call(0, scal, ints, meta, samples, below, above, None, ws, stages[:1], tile_value, early)
    for section in range(1, SEG):
        sender, head, tail = sender_call(section, scal, h, w_source, stages)
        below = lax.ppermute(tail, "dom", to_dom(1))
        above = lax.ppermute(head, "dom", to_dom(-1))
        h = section_call(section, scal, ints, meta, h, below, above, sender, ws, stages, tile_value, moved)
    return h[None]


def solution(mesh):
    return jax.shard_map(
        shards,
        mesh=mesh,
        in_specs=(
            P(None, "dom", None),
            P("segment", None, None, None),
            P("segment", None, None, None),
            P("segment", None, None, None),
            P("segment", None, None, None),
            P("segment", None, None),
            P("segment", "dom", None),
            P("segment", "dom"),
            P("segment", "dom", None, None, None),
        ),
        out_specs=P("segment", "dom", None),
        check_vma=False,
    )
```

```python
import functools

import jax
import jax.numpy as jnp
from jax import lax
from jax.experimental import pallas as pl
from jax.experimental.pallas import tpu as pltpu
from jax.sharding import PartitionSpec as P

D = 512
BLK = 128
BD = 4
K = 6
SEG = 4
Y, Z = 4, 8
HALF = D // 2
META = 16
ROWS = 2 * K * BLK
BF = jnp.bfloat16
F32 = jnp.float32
ANY = pl.BlockSpec(memory_space=pl.ANY)
HBM = pl.BlockSpec(memory_space=pltpu.HBM)
SMEM = pl.BlockSpec(memory_space=pltpu.SMEM)
VMEM = pl.BlockSpec(memory_space=pltpu.VMEM)


def silu(v):
    return (0.5 * v) * (1.0 + jnp.tanh(0.5 * v))


def params(mib):
    return pltpu.CompilerParams(vmem_limit_bytes=mib * 2**20)


def by_segment(x):
    return [(i, i ^ x) for i in range(SEG)]


def dom_pairs(move):
    out = []
    for d in range(Z * Y * 2):
        z, y, c = move(d // (2 * Y), d // 2 % Y, d % 2)
        out.append((d, ((z % Z) * Y + y % Y) * 2 + c % 2))
    return out


def by_y(x):
    return dom_pairs(lambda z, y, c: (z, y ^ x, c))


Z_EVEN = dom_pairs(lambda z, y, c: (z ^ 1, y, c))
Z_ODD = dom_pairs(lambda z, y, c: (((z + 1) ^ 1) - 1, y, c))
OTHER_CORE = dom_pairs(lambda z, y, c: (z, y, c ^ 1))
NEXT_CHIP = [(d, (((d + 1) ^ 1) - 1) % (2 * Y * Z)) for d in range(2 * Y * Z)]


def place():
    p, dom = lax.axis_index("segment"), lax.axis_index("dom")
    return p, dom, (dom >> 1) & 3, (dom >> 3) & 1, dom & 1


def meta_kernel(src, cnt, gain, out):
    dom = place()[1]
    row = lax.broadcasted_iota(jnp.int32, (META, BLK), 0)
    col = lax.broadcasted_iota(jnp.int32, (META, BLK), 1)
    meta = jnp.zeros((META, BLK), F32)
    for b in range(BD):
        for k in range(K):
            rel = (src[0, b, k] - (dom * BD - 1) + 512) & 255
            code = jnp.where(k < cnt[0, b], rel, 7).astype(F32)
            meta = jnp.where((row == 0) & (col == b * K + k), code, meta)
    left = gain[0]
    for part in range(3):
        piece = left.astype(BF).astype(F32)
        left = left - piece
        for i in range(4):
            meta = jnp.where(row == 1 + 4 * part + i, piece[:, i * BLK : (i + 1) * BLK], meta)
    out[...] = meta.astype(BF)


def meta_call(src, cnt, gain):
    return pl.pallas_call(
        meta_kernel,
        out_shape=jax.ShapeDtypeStruct((META, BLK), BF),
        in_specs=[SMEM, SMEM, VMEM],
        out_specs=VMEM,
        compiler_params=params(4),
        name="meta",
    )(src, cnt, gain)


def copies(kernel_name, plan, shapes, *args):
    def kernel(*refs):
        ins, outs, sem = refs[: len(args)], refs[len(args) : -1], refs[-1]
        moves = [
            pltpu.make_async_copy(a, b, sem.at[i]) for i, (a, b) in enumerate(plan(ins, outs))
        ]
        for m in moves:
            m.start()
        for m in moves:
            m.wait()

    return pl.pallas_call(
        kernel,
        out_shape=[jax.ShapeDtypeStruct(shape, BF) for shape in shapes],
        in_specs=[ANY] * len(args),
        out_specs=[ANY] * len(shapes),
        scratch_shapes=[pltpu.SemaphoreType.DMA((12,))],
        compiler_params=params(4),
        cost_estimate=pl.CostEstimate(flops=0, bytes_accessed=2_000_000, transcendentals=0),
        name=kernel_name,
    )(*args)


def z_halves(ring):
    def plan(ins, outs):
        return [
            (ins[r].at[pl.ds(i * BLK, BLK)], outs[i].at[r]) for r in range(4) for i in range(2)
        ]

    return copies("halves", plan, [(4, BLK, HALF)] * 2, *ring)


def joined(ring, halves):
    def plan(ins, outs):
        return [(ins[r], outs[0].at[r]) for r in range(4)] + [
            (ins[4 + i], outs[0].at[pl.ds(4, 4), pl.ds(i * BLK, BLK)]) for i in range(2)
        ]

    return copies("joined", plan, [(8, HALF, HALF)], *ring, *halves)[0]


def weights_kernel(section, holders, n_stage, *refs):
    own, stages = refs[:4], [refs[4 + 2 * j : 6 + 2 * j] for j in range(n_stage)]
    out, sem = refs[-2:]
    p, _, y, zpar, c = place()

    @pl.when(p == section)
    def _():
        for m in range(4):
            pltpu.make_async_copy(own[m].at[0, 0], out.at[m], sem.at[m]).start()

    for (first, second), held_by in zip(stages, holders):

        @pl.when(functools.reduce(jnp.logical_or, [p == q for q in held_by]))
        def _():
            for m in range(4):
                for core, stage in enumerate((first, second)):
                    for zrel in range(2):
                        rows = pl.multiple_of((zpar ^ zrel) * HALF, HALF)
                        cols = pl.multiple_of((c ^ core) * HALF, HALF)
                        pltpu.make_async_copy(
                            stage.at[zrel * 4 + (y ^ m)],
                            out.at[m, pl.ds(rows, HALF), pl.ds(cols, HALF)],
                            sem.at[m],
                        ).start()

    for m in range(4):
        pltpu.make_async_copy(own[m].at[0, 0], out.at[m], sem.at[m]).wait()


def weights_call(section, own, stages):
    by_stage = {}
    for q in range(SEG):
        if q != section:
            by_stage.setdefault(section - (1 if section > q else 0), []).append(q)
    flat = [a for j in by_stage for a in stages[j]]
    return pl.pallas_call(
        functools.partial(weights_kernel, section, list(by_stage.values()), len(by_stage)),
        out_shape=jax.ShapeDtypeStruct((4, D, D), BF),
        in_specs=[ANY] * (4 + len(flat)),
        out_specs=VMEM,
        scratch_shapes=[pltpu.SemaphoreType.DMA((4,))],
        compiler_params=params(4),
        cost_estimate=pl.CostEstimate(flops=0, bytes_accessed=4_000_000, transcendentals=0),
        name=f"weights{section}",
    )(*own, *flat)


def tile_halves(section, p):
    x = p ^ section
    if x == 0:
        return "own_a", "own_b"
    if x == 1:
        return "r1a", ("r2a" if p == 1 else "r3a")
    if x == 2:
        return ("r3c" if p == 3 else "r2c"), ("r3a" if p == 1 else "r2a")
    return ("r2c" if p == 3 else "r3c"), "r1c"


def tiles_kernel(section, names, *refs):
    ins = dict(zip(names, refs))
    tiles, codes, gain, meta, sem = refs[len(names) :]
    for q in range(SEG):

        @pl.when(lax.axis_index("segment") == q)
        def _():
            a, b = (ins[name] for name in tile_halves(section, q))
            for i in range(2 * K):
                rows = pl.ds(i * BLK, BLK)
                pltpu.make_async_copy(a.at[rows], tiles.at[i], sem.at[0]).start()
                pltpu.make_async_copy(b.at[rows], tiles.at[2 * K + i], sem.at[1]).start()
            pltpu.make_async_copy(a.at[pl.ds(ROWS, META)], meta, sem.at[2]).start()

    pltpu.make_async_copy(ins["own_a"].at[pl.ds(ROWS, META)], meta, sem.at[2]).wait()
    for half in range(2):
        there = tiles.at[pl.ds(half * 2 * K, 2 * K)]
        pltpu.make_async_copy(there, there, sem.at[half]).wait()
    m = meta[...].astype(F32)
    code = m[:8]
    codes[...] = jnp.where(code < 7.0, code, 0.0).astype(jnp.int32)
    gain[...] = jnp.concatenate(
        [m[1 + i : 2 + i] + (m[5 + i : 6 + i] + m[9 + i : 10 + i]) for i in range(4)], axis=1
    )
    for i in range(BD * K):
        used = jnp.broadcast_to(m[0:1, i : i + 1], (BLK, BLK)) < 7.0
        tiles[i] = jnp.where(used, tiles[i].astype(F32), 0.0).astype(BF)


def tiles_call(section, arrays):
    return pl.pallas_call(
        functools.partial(tiles_kernel, section, list(arrays)),
        out_shape=[
            jax.ShapeDtypeStruct((BD * K, BLK, BLK), BF),
            jax.ShapeDtypeStruct((8, BLK), jnp.int32),
            jax.ShapeDtypeStruct((1, D), F32),
        ],
        in_specs=[ANY] * len(arrays),
        out_specs=[VMEM] * 3,
        scratch_shapes=[pltpu.VMEM((META, BLK), BF), pltpu.SemaphoreType.DMA((3,))],
        compiler_params=params(4),
        cost_estimate=pl.CostEstimate(flops=0, bytes_accessed=2_000_000, transcendentals=0),
        name=f"tiles{section}",
    )(*arrays.values())


def section_kernel(section, codes, gain, tiles, w, h, inner, outer, *rest):
    sender = rest[0]
    out, sbuf, gbuf = rest[-3:]
    core = place()[4]
    at_inner = pl.multiple_of((1 - core) * (5 * BLK), BLK)
    at_outer = pl.multiple_of(core * (5 * BLK), BLK)
    if section == 0:
        for at, src in ((at_inner, inner), (at_outer, outer)):
            s = silu(jnp.dot(src[...], w[0], preferred_element_type=F32)).astype(BF)
            sbuf[pl.ds(at, BLK), :] = s
        for i in range(2):
            s = jnp.dot(h[i * HALF : (i + 1) * HALF, :], w[0], preferred_element_type=F32)
            sbuf[BLK + i * HALF : BLK + (i + 1) * HALF, :] = silu(s).astype(BF)
    else:
        sbuf[BLK : 5 * BLK, :] = sender[...]
        sbuf[pl.ds(at_inner, BLK), :] = inner[...]
        sbuf[pl.ds(at_outer, BLK), :] = outer[...]
    for b in range(BD):
        places = [pl.multiple_of(codes[0, b * K + k] * BLK, BLK) for k in range(K)]
        got = jnp.dot(
            jnp.concatenate([tiles[b * K + k] for k in range(K)], axis=1),
            jnp.concatenate([sbuf[pl.ds(at, BLK), :] for at in places], axis=0),
            preferred_element_type=F32,
        )
        gbuf[b * BLK : (b + 1) * BLK, :] = got.astype(BF)
    for i in range(2):
        rows = slice(i * HALF, (i + 1) * HALF)
        mixed = jnp.dot(h[rows, :], w[1], preferred_element_type=F32)
        mixed = mixed + jnp.dot(gbuf[rows, :], w[2], preferred_element_type=F32)
        mean = jnp.mean(mixed * mixed, axis=-1, keepdims=True)
        scaled = mixed * lax.rsqrt(mean + 1e-05) * gain[...]
        update = silu(scaled).astype(BF)
        new = h[rows, :].astype(F32) + jnp.dot(update, w[3], preferred_element_type=F32)
        out[rows, :] = new.astype(BF)


def section_call(section, codes, gain, tiles, w, h, inner, outer, *sender):
    return pl.pallas_call(
        functools.partial(section_kernel, section),
        out_shape=jax.ShapeDtypeStruct((BD * BLK, D), BF),
        in_specs=[SMEM] + [VMEM] * (6 + len(sender)),
        out_specs=VMEM,
        scratch_shapes=[
            pltpu.VMEM(((BD + 2) * BLK, D), BF),
            pltpu.VMEM((BD * BLK, D), BF),
        ],
        compiler_params=params(16),
        cost_estimate=pl.CostEstimate(
            flops=1_500_000_000, bytes_accessed=4_000_000, transcendentals=262144
        ),
        name=f"section{section}",
    )(codes, gain, tiles, w, h, inner, outer, *sender)


def sender_kernel(h, w, full, inner, outer):
    core = place()[4]
    for i in range(2):
        rows = slice(i * HALF, (i + 1) * HALF)
        s = silu(jnp.dot(h[rows, :], w[0], preferred_element_type=F32)).astype(BF)
        full[rows, :] = s
    inner[...] = full[pl.ds(pl.multiple_of((1 - core) * 3 * BLK, BLK), BLK), :]
    outer[...] = full[pl.ds(pl.multiple_of(core * 3 * BLK, BLK), BLK), :]


def sender_call(section, h, w):
    return pl.pallas_call(
        sender_kernel,
        out_shape=[
            jax.ShapeDtypeStruct((BD * BLK, D), BF),
            jax.ShapeDtypeStruct((BLK, D), BF),
            jax.ShapeDtypeStruct((BLK, D), BF),
        ],
        in_specs=[VMEM, VMEM],
        out_specs=[VMEM] * 3,
        compiler_params=params(8),
        cost_estimate=pl.CostEstimate(
            flops=270_000_000, bytes_accessed=1_500_000, transcendentals=262144
        ),
        name=f"sender{section}",
    )(h, w)


def after(values, *others):
    return lax.optimization_barrier((values, others))[0]


def over_segments(value, x):
    return lax.ppermute(value, "segment", by_segment(x))


def over_dom(value, pairs):
    return lax.ppermute(value, "dom", pairs)


def exchange(inner, outer):
    return over_dom(inner, OTHER_CORE), over_dom(outer, NEXT_CHIP)


def shards(samples, w_source, w_self, w_message, w_output, norm_gain, tile_source, tile_count, tile_value):
    p, _, y, zpar, core = place()
    ws = [w_source, w_self, w_message, w_output]
    piece = [lax.dynamic_slice(w[0, 0], (zpar * HALF, core * HALF), (HALF, HALF)) for w in ws]
    piece = jnp.where(
        y < 2, jnp.where(y == 0, piece[0], piece[1]), jnp.where(y == 2, piece[2], piece[3])
    )
    x1, x3 = over_segments(piece, 1), over_segments(piece, 3)
    x2 = over_segments(piece, 2)

    h = lax.dynamic_index_in_dim(samples, p, 0, keepdims=False)
    edge = [h[:BLK], h[(BD - 1) * BLK :]]
    inner, outer = exchange(
        jnp.where(core == 0, edge[1], edge[0]), jnp.where(core == 0, edge[0], edge[1])
    )

    root = p == 0
    half_a, half_b = tile_value[0, :2].reshape(ROWS, BLK), tile_value[0, 2:].reshape(ROWS, BLK)
    half_a = jnp.concatenate([half_a, meta_call(tile_source, tile_count, norm_gain)])
    arrays = {"own_a": half_a, "own_b": half_b}
    half_a, half_b = after((half_a, half_b), x1, x3, inner, outer)
    arrays["r1a"], arrays["r1c"] = over_segments(half_a, 1), over_segments(half_b, 3)
    second = (jnp.where(root, half_b, arrays["r1c"]), jnp.where(root, half_a, arrays["r1a"]))
    arrays["r2a"], arrays["r2c"] = over_segments(second[0], 1), over_segments(second[1], 3)
    early = dict(arrays)
    half_a, half_b = after((half_a, half_b), arrays["r2a"], arrays["r2c"])
    third = (jnp.where(root, arrays["r1c"], half_b), jnp.where(root, arrays["r1a"], half_a))
    arrays["r3a"], arrays["r3c"] = over_segments(third[0], 1), over_segments(third[1], 3)

    pieces = [
        jnp.where(p == 2, x2, jnp.where(p == 3, x3, x1)),
        jnp.where((p == 0) | (p == 3), x2, x3),
        jnp.where(p == 0, x3, jnp.where(p == 1, x2, x1)),
    ]

    def over_y(own):
        a, b = over_dom(own, by_y(1)), over_dom(own, by_y(3))
        return [own, a, over_dom(own, by_y(2)), b]

    def over_z(halves):
        return over_dom(halves[0], Z_EVEN), over_dom(halves[1], Z_ODD)

    def both(pieces):
        return pieces, over_dom(pieces, OTHER_CORE)

    ring0 = over_y(pieces[0])
    z0 = over_z(z_halves(ring0))
    ring1 = over_y(after(pieces[1], ring0, arrays["r1a"], arrays["r1c"]))
    stage0 = both(after(joined(ring0, z0), second))
    z1 = over_z(after(z_halves(ring1), z0))
    w = weights_call(0, ws, [stage0])
    tiles, codes, gain = tiles_call(0, early)
    h = section_call(0, codes, gain, tiles, w, h, inner, outer)
    stage1 = both(after(joined(ring1, z1), third))
    ring2 = over_y(after(pieces[2], z1))
    z2 = over_z(z_halves(after(ring2, h)))
    stage2 = both(joined(ring2, z2))
    stages = [stage0, stage1, stage2]
    for section in range(1, SEG):
        w = weights_call(section, ws, stages)
        tiles, codes, gain = tiles_call(section, arrays)
        sender, inner, outer = sender_call(section, h, w)
        inner, outer = exchange(inner, outer)
        h = section_call(section, codes, gain, tiles, w, h, inner, outer, sender)
    return h[None]


def solution(mesh):
    return jax.shard_map(
        shards,
        mesh=mesh,
        in_specs=(
            P(None, "dom", None),
            P("segment", None, None, None),
            P("segment", None, None, None),
            P("segment", None, None, None),
            P("segment", None, None, None),
            P("segment", None, None),
            P("segment", "dom", None),
            P("segment", "dom"),
            P("segment", "dom", None, None, None),
        ),
        out_specs=P("segment", "dom", None),
        check_vma=False,
    )
```

```python
import functools

import jax
import jax.numpy as jnp
from jax import lax
from jax.experimental import pallas as pl
from jax.experimental.pallas import tpu as pltpu
from jax.sharding import PartitionSpec as P

D = 512
BLK = 128
BD = 4
K = 6
SEG = 4
Y, Z = 4, 8
HALF = D // 2
META = 16
ROWS = 2 * K * BLK
BF = jnp.bfloat16
F32 = jnp.float32
ANY = pl.BlockSpec(memory_space=pl.ANY)
HBM = pl.BlockSpec(memory_space=pltpu.HBM)
SMEM = pl.BlockSpec(memory_space=pltpu.SMEM)
VMEM = pl.BlockSpec(memory_space=pltpu.VMEM)


def silu(v):
    return (0.5 * v) * (1.0 + jnp.tanh(0.5 * v))


def params(mib):
    return pltpu.CompilerParams(vmem_limit_bytes=mib * 2**20)


def by_segment(x):
    return [(i, i ^ x) for i in range(SEG)]


def dom_pairs(move):
    out = []
    for d in range(Z * Y * 2):
        z, y, c = move(d // (2 * Y), d // 2 % Y, d % 2)
        out.append((d, ((z % Z) * Y + y % Y) * 2 + c % 2))
    return out


def by_y(x):
    return dom_pairs(lambda z, y, c: (z, y ^ x, c))


Z_FAR = dom_pairs(lambda z, y, c: (z ^ 2, y, c))
Z_EVEN = dom_pairs(lambda z, y, c: (z ^ 1, y, c))
Z_ODD = dom_pairs(lambda z, y, c: (((z + 1) ^ 1) - 1, y, c))
OTHER_CORE = dom_pairs(lambda z, y, c: (z, y, c ^ 1))
NEXT_CHIP = [(d, (((d + 1) ^ 1) - 1) % (2 * Y * Z)) for d in range(2 * Y * Z)]


def place():
    p, dom = lax.axis_index("segment"), lax.axis_index("dom")
    return p, dom, (dom >> 1) & 3, (dom >> 3) & 1, dom & 1


def sender_rows(rows, w):
    return silu(jnp.dot(rows, w, preferred_element_type=F32)).astype(BF)


def halo_places():
    core = place()[4]
    return pl.multiple_of((1 - core) * (5 * BLK), BLK), pl.multiple_of(core * (5 * BLK), BLK)


def gather(tile, code, sbuf, gbuf):
    for b in range(BD):
        slots = range(b * K, (b + 1) * K)
        places = [pl.multiple_of(code(i) * BLK, BLK) for i in slots]
        got = jnp.dot(
            jnp.concatenate([tile(i) for i in slots], axis=1),
            jnp.concatenate([sbuf[pl.ds(at, BLK), :] for at in places], axis=0),
            preferred_element_type=F32,
        )
        gbuf[b * BLK : (b + 1) * BLK, :] = got.astype(BF)


def update_rows(h, gathered, w, gain):
    mixed = jnp.dot(h, w[1], preferred_element_type=F32)
    mixed = mixed + jnp.dot(gathered, w[2], preferred_element_type=F32)
    mean = jnp.mean(mixed * mixed, axis=-1, keepdims=True)
    update = silu(mixed * lax.rsqrt(mean + 1e-05) * gain).astype(BF)
    return (h.astype(F32) + jnp.dot(update, w[3], preferred_element_type=F32)).astype(BF)


def own_small(src, cnt, gain):
    dom = place()[1]
    row = lax.broadcasted_iota(jnp.int32, (META, BLK), 0)
    col = lax.broadcasted_iota(jnp.int32, (META, BLK), 1)
    meta = jnp.zeros((META, BLK), F32)
    for i in range(BD * K):
        used, code = own_slot(src, cnt, dom, i)
        meta = jnp.where((row == 0) & (col == i), jnp.where(used, code, 7).astype(F32), meta)
    left = gain[0]
    for part in range(3):
        piece = left.astype(BF).astype(F32)
        left = left - piece
        for i in range(4):
            meta = jnp.where(row == 1 + 4 * part + i, piece[:, i * BLK : (i + 1) * BLK], meta)
    return meta.astype(BF)


def own_slot(src, cnt, dom, i):
    b, k = divmod(i, K)
    return k < cnt[0, b], (src[0, b, k] - (dom * BD - 1) + 512) & 255


def first_kernel(order, src, cnt, gain, inner, outer, samples, w0, w1, w2, w3, tiles, *rest):
    outs, (wbuf, tbuf, sbuf, gbuf, hbuf, ibuf, obuf, wsem, tsem, hsem, esem) = rest[:-11], rest[-11:]
    p, dom, _, _, _ = place()

    @pl.when(p == 0)
    def _():
        for m, w in enumerate((w0, w1, w2, w3)):
            pltpu.make_async_copy(w.at[0, 0], wbuf.at[m], wsem.at[m]).start()
        for n, sample in enumerate(order):
            pltpu.make_async_copy(samples.at[sample], hbuf.at[n], hsem.at[n]).start()
            pltpu.make_async_copy(inner.at[sample], ibuf.at[n], esem.at[0, n]).start()
            pltpu.make_async_copy(outer.at[sample], obuf.at[n], esem.at[1, n]).start()
        pltpu.make_async_copy(tiles.at[0], tbuf, tsem).start()
        in_place = halo_places()

        def tile(i):
            b, k = divmod(i, K)
            used, _ = own_slot(src, cnt, dom, i)
            t = tbuf[b, k]
            return jnp.where(used, t, jnp.zeros_like(t))

        def code(i):
            used, at = own_slot(src, cnt, dom, i)
            return jnp.where(used, at, 0)

        for n, sample in enumerate(order):
            if n == 0:
                pltpu.make_async_copy(w0.at[0, 0], wbuf.at[0], wsem.at[0]).wait()
            pltpu.make_async_copy(samples.at[sample], hbuf.at[n], hsem.at[n]).wait()
            pltpu.make_async_copy(inner.at[sample], ibuf.at[n], esem.at[0, n]).wait()
            pltpu.make_async_copy(outer.at[sample], obuf.at[n], esem.at[1, n]).wait()
            for at, block in zip(in_place, (ibuf, obuf)):
                sbuf[pl.ds(at, BLK), :] = sender_rows(block[n], wbuf[0])
            for i in range(2):
                rows = slice(i * HALF, (i + 1) * HALF)
                sbuf[BLK + i * HALF : BLK + (i + 1) * HALF, :] = sender_rows(hbuf[n, rows, :], wbuf[0])
            if n == 0:
                pltpu.make_async_copy(tiles.at[0], tbuf, tsem).wait()
                for m, w in ((1, w1), (2, w2), (3, w3)):
                    pltpu.make_async_copy(w.at[0, 0], wbuf.at[m], wsem.at[m]).wait()
            gather(tile, code, sbuf, gbuf)
            for i in range(2):
                rows = slice(i * HALF, (i + 1) * HALF)
                new = update_rows(hbuf[n, rows, :], gbuf[rows, :], wbuf, gain[0])
                if sample == 0:
                    outs[0][rows, :] = new
                    continue
                for j in range(4):
                    which, at = layout(sample, j)
                    outs[which][at + i * HALF : at + (i + 1) * HALF, :] = new[:, j * BLK : (j + 1) * BLK]

    if 0 not in order:

        @pl.when(p != 0)
        def _():
            moves = [
                pltpu.make_async_copy(
                    tiles.at[0, b, k], out.at[pl.ds((b * K + k) * BLK, BLK)], wsem.at[n]
                )
                for n, out in enumerate(outs)
                for b in range(BD)
                for k in range(K)
            ]
            for m in moves:
                m.start()
            small = own_small(src, cnt, gain)
            for n, out in enumerate(outs):
                out[2 * ROWS :, :] = small
                there = out.at[pl.ds(0, 2 * ROWS)]
                pltpu.make_async_copy(there, there, wsem.at[n]).wait()


def layout(sample, j):
    if sample == 1:
        return 0, 2 * D + j * D
    if sample == 3:
        return 1, j * D
    return (0, j * D) if j < 2 else (1, 4 * D + (j - 2) * D)


def first_call(order, src, cnt, gain, inner, outer, samples, ws, tiles):
    n = len(order)
    shape = (D, D) if 0 in order else (2 * ROWS + META, BLK)
    return pl.pallas_call(
        functools.partial(first_kernel, order),
        out_shape=[jax.ShapeDtypeStruct(shape, BF)] * (1 if 0 in order else 2),
        in_specs=[SMEM, SMEM, VMEM] + [ANY] * 8,
        out_specs=[VMEM] * (1 if 0 in order else 2),
        scratch_shapes=[
            pltpu.VMEM((4, D, D), BF),
            pltpu.VMEM((BD, K, BLK, BLK), BF),
            pltpu.VMEM(((BD + 2) * BLK, D), BF),
            pltpu.VMEM((BD * BLK, D), BF),
            pltpu.VMEM((n, D, D), BF),
            pltpu.VMEM((n, BLK, D), BF),
            pltpu.VMEM((n, BLK, D), BF),
            pltpu.SemaphoreType.DMA((4,)),
            pltpu.SemaphoreType.DMA,
            pltpu.SemaphoreType.DMA((n,)),
            pltpu.SemaphoreType.DMA((2, n)),
        ],
        compiler_params=params(20 if 0 in order else 60),
        cost_estimate=pl.CostEstimate(
            flops=2_000_000_000 * n, bytes_accessed=4_000_000, transcendentals=262144 * n
        ),
        name=f"first{n}",
    )(src, cnt, gain, inner, outer, samples, *ws, tiles)


def arrived_kernel(h0, near, far, mixed_a, mixed_b, out, sem):
    p = lax.axis_index("segment")

    @pl.when(p == 0)
    def _():
        pltpu.make_async_copy(h0, out, sem).start()

    for q in (1, 2, 3):

        @pl.when(p == q)
        def _():
            for j in range(4):
                which, at = layout(q, j)
                src = (near, far)[which]
                if q == 2:
                    src, at = (mixed_a, at) if which == 0 else (mixed_b, at - ROWS)
                pltpu.make_async_copy(
                    src.at[pl.ds(at, D)], out.at[:, pl.ds(j * BLK, BLK)], sem
                ).start()

    pltpu.make_async_copy(h0, out, sem).wait()


def arrived_call(*args):
    return pl.pallas_call(
        arrived_kernel,
        out_shape=jax.ShapeDtypeStruct((D, D), BF),
        in_specs=[ANY] * 5,
        out_specs=VMEM,
        scratch_shapes=[pltpu.SemaphoreType.DMA],
        compiler_params=params(4),
        name="arrived",
    )(*args)


def copies(kernel_name, plan, shapes, *args):
    def kernel(*refs):
        ins, outs, sem = refs[: len(args)], refs[len(args) : -1], refs[-1]
        moves = [
            pltpu.make_async_copy(a, b, sem.at[i]) for i, (a, b) in enumerate(plan(ins, outs))
        ]
        for m in moves:
            m.start()
        for m in moves:
            m.wait()

    return pl.pallas_call(
        kernel,
        out_shape=[jax.ShapeDtypeStruct(shape, BF) for shape in shapes],
        in_specs=[ANY] * len(args),
        out_specs=[ANY] * len(shapes),
        scratch_shapes=[pltpu.SemaphoreType.DMA((12,))],
        compiler_params=params(4),
        cost_estimate=pl.CostEstimate(flops=0, bytes_accessed=2_000_000, transcendentals=0),
        name=kernel_name,
    )(*args)


def joined(ring):
    def plan(ins, outs):
        return [(ins[r], outs[0].at[r]) for r in range(4)]

    return copies("joined", plan, [(4, D, HALF)], *ring)[0]


STAGE_BY_Y = {1: True, 2: False, 3: True}


def weights_kernel(section, *refs):
    own, stage = refs[:4], refs[4:6]
    out, sem = refs[-2:]
    p, dom, y, _, c = place()

    @pl.when(p == section)
    def _():
        for m in range(4):
            pltpu.make_async_copy(own[m].at[0, 0], out.at[m], sem.at[m]).start()

    @pl.when(p != section)
    def _():
        first = y if STAGE_BY_Y[section] else (dom >> 3) & 3
        for m in range(4):
            for core in range(2):
                cols = pl.multiple_of((c ^ core) * HALF, HALF)
                pltpu.make_async_copy(
                    stage[core].at[first ^ m], out.at[m, :, pl.ds(cols, HALF)], sem.at[m]
                ).start()

    for m in range(4):
        pltpu.make_async_copy(own[m].at[0, 0], out.at[m], sem.at[m]).wait()


def weights_call(section, own, stage):
    return pl.pallas_call(
        functools.partial(weights_kernel, section),
        out_shape=jax.ShapeDtypeStruct((4, D, D), BF),
        in_specs=[ANY] * 6,
        out_specs=VMEM,
        scratch_shapes=[pltpu.SemaphoreType.DMA((4,))],
        compiler_params=params(4),
        cost_estimate=pl.CostEstimate(flops=0, bytes_accessed=4_000_000, transcendentals=0),
        name=f"weights{section}",
    )(*own, *stage)


def tiles_kernel(section, own, near, far, mixed_a, mixed_b, tiles, codes, gain, meta, sem):
    for q in range(SEG):

        @pl.when(lax.axis_index("segment") == q)
        def _():
            x = q ^ section
            if x == 2:
                first, second, small = mixed_a, mixed_b, mixed_b.at[pl.ds(ROWS, META)]
            else:
                whole = {0: own, 1: near, 3: far}[x]
                first, second = whole, whole.at[pl.ds(ROWS, ROWS)]
                small = whole.at[pl.ds(2 * ROWS, META)]
            for i in range(2 * K):
                rows = pl.ds(i * BLK, BLK)
                pltpu.make_async_copy(first.at[rows], tiles.at[i], sem.at[0]).start()
                pltpu.make_async_copy(second.at[rows], tiles.at[2 * K + i], sem.at[1]).start()
            pltpu.make_async_copy(small, meta, sem.at[2]).start()

    pltpu.make_async_copy(own.at[pl.ds(2 * ROWS, META)], meta, sem.at[2]).wait()
    for half in range(2):
        there = tiles.at[pl.ds(half * 2 * K, 2 * K)]
        pltpu.make_async_copy(there, there, sem.at[half]).wait()
    m = meta[...].astype(F32)
    code = m[:8]
    codes[...] = jnp.where(code < 7.0, code, 0.0).astype(jnp.int32)
    gain[...] = jnp.concatenate(
        [m[1 + i : 2 + i] + (m[5 + i : 6 + i] + m[9 + i : 10 + i]) for i in range(4)], axis=1
    )
    for i in range(BD * K):
        used = jnp.broadcast_to(m[0:1, i : i + 1], (BLK, BLK)) < 7.0
        tiles[i] = jnp.where(used, tiles[i].astype(F32), 0.0).astype(BF)


def tiles_call(section, arrays):
    return pl.pallas_call(
        functools.partial(tiles_kernel, section),
        out_shape=[
            jax.ShapeDtypeStruct((BD * K, BLK, BLK), BF),
            jax.ShapeDtypeStruct((8, BLK), jnp.int32),
            jax.ShapeDtypeStruct((1, D), F32),
        ],
        in_specs=[ANY] * len(arrays),
        out_specs=[VMEM] * 3,
        scratch_shapes=[pltpu.VMEM((META, BLK), BF), pltpu.SemaphoreType.DMA((3,))],
        compiler_params=params(4),
        cost_estimate=pl.CostEstimate(flops=0, bytes_accessed=2_000_000, transcendentals=0),
        name=f"tiles{section}",
    )(*arrays)


def section_kernel(codes, gain, tiles, w, h, inner, outer, sender, out, sbuf, gbuf):
    sbuf[BLK : 5 * BLK, :] = sender[...]
    for at, block in zip(halo_places(), (inner, outer)):
        sbuf[pl.ds(at, BLK), :] = block[...]
    gather(lambda i: tiles[i], lambda i: codes[0, i], sbuf, gbuf)
    for i in range(2):
        rows = slice(i * HALF, (i + 1) * HALF)
        out[rows, :] = update_rows(h[rows, :], gbuf[rows, :], w, gain[...])


def section_call(section, codes, gain, tiles, w, h, inner, outer, sender):
    return pl.pallas_call(
        section_kernel,
        out_shape=jax.ShapeDtypeStruct((BD * BLK, D), BF),
        in_specs=[SMEM] + [VMEM] * 7,
        out_specs=VMEM,
        scratch_shapes=[
            pltpu.VMEM(((BD + 2) * BLK, D), BF),
            pltpu.VMEM((BD * BLK, D), BF),
        ],
        compiler_params=params(16),
        cost_estimate=pl.CostEstimate(
            flops=1_500_000_000, bytes_accessed=4_000_000, transcendentals=262144
        ),
        name=f"section{section}",
    )(codes, gain, tiles, w, h, inner, outer, sender)


def sender_kernel(h, w, full, inner, outer):
    core = place()[4]
    for i in range(2):
        rows = slice(i * HALF, (i + 1) * HALF)
        full[rows, :] = sender_rows(h[rows, :], w[0])
    inner[...] = full[pl.ds(pl.multiple_of((1 - core) * 3 * BLK, BLK), BLK), :]
    outer[...] = full[pl.ds(pl.multiple_of(core * 3 * BLK, BLK), BLK), :]


def sender_call(section, h, w):
    return pl.pallas_call(
        sender_kernel,
        out_shape=[
            jax.ShapeDtypeStruct((BD * BLK, D), BF),
            jax.ShapeDtypeStruct((BLK, D), BF),
            jax.ShapeDtypeStruct((BLK, D), BF),
        ],
        in_specs=[VMEM, VMEM],
        out_specs=[VMEM] * 3,
        compiler_params=params(8),
        cost_estimate=pl.CostEstimate(
            flops=270_000_000, bytes_accessed=1_500_000, transcendentals=262144
        ),
        name=f"sender{section}",
    )(h, w)


def after(values, *others):
    return lax.optimization_barrier((values, others))[0]


def over_segments(value, x):
    return lax.ppermute(value, "segment", by_segment(x))


def over_dom(value, pairs):
    return lax.ppermute(value, "dom", pairs)


def exchange(inner, outer):
    return over_dom(inner, OTHER_CORE), over_dom(outer, NEXT_CHIP)


def shards(samples, w_source, w_self, w_message, w_output, norm_gain, tile_source, tile_count, tile_value):
    p, dom, y, _, core = place()
    ws = [w_source, w_self, w_message, w_output]
    edge = [samples[:, :BLK], samples[:, (BD - 1) * BLK :]]
    edge = [jnp.where(core == 0, edge[1], edge[0]), jnp.where(core == 0, edge[0], edge[1])]
    inner, outer = exchange(*edge)

    m = jnp.where(p == 2, (dom >> 3) & 3, y)
    a, b, c, d = (lax.dynamic_slice(w[0, 0], (0, core * HALF), (D, HALF)) for w in ws)
    piece = jnp.where(m < 2, jnp.where(m == 0, a, b), jnp.where(m == 2, c, d))
    piece = after(piece, edge)
    x1, x3, x2 = over_segments(piece, 1), over_segments(piece, 3), over_segments(piece, 2)

    small = (tile_source, tile_count, norm_gain, inner, outer, samples, ws, tile_value)
    own, own_far = first_call((2, 1, 3), *small)
    near, far = over_segments(own, 1), over_segments(own_far, 3)
    (h0,) = first_call((0,), *small)
    mixed_b, mixed_a = over_segments(far[ROWS:], 1), over_segments(near[:ROWS], 3)
    arrays = [own, near, far, mixed_a, mixed_b]

    def ring(own, routes, *waits):
        a, c = over_dom(own, routes[0]), over_dom(own, routes[2])
        b = over_dom(after(own, a, c, waits), routes[1])
        return [own, a, b, c]

    def both(pieces):
        return pieces, over_dom(pieces, OTHER_CORE)

    over_y, over_z = [by_y(x) for x in (1, 2, 3)], [Z_EVEN, Z_FAR, Z_ODD]
    x1, x2, x3 = after((x1, x2, x3), own, own_far)
    ring1 = ring(jnp.where(p == 2, x3, jnp.where(p == 3, x2, x1)), over_y)
    then = jnp.where(p == 0, x2, jnp.where(p == 1, x3, x1))
    last = jnp.where(p == 0, x3, jnp.where(p == 1, x2, x1))
    then, last = after((then, last), near, far, ring1)
    ring2, ring3 = ring(then, over_z), ring(last, over_y)
    stages = {1: both(joined(ring1)), 2: both(joined(ring2))}
    h = arrived_call(h0, near, far, mixed_a, mixed_b)
    for section in range(1, SEG):
        if section == 2:
            stages[3] = both(joined(after(ring3, h)))
        w = weights_call(section, ws, stages[section])
        tiles, codes, gain = tiles_call(section, arrays)
        sender, inner, outer = sender_call(section, h, w)
        inner, outer = exchange(inner, outer)
        h = section_call(section, codes, gain, tiles, w, h, inner, outer, sender)
    return h[None]


def solution(mesh):
    return jax.shard_map(
        shards,
        mesh=mesh,
        in_specs=(
            P(None, "dom", None),
            P("segment", None, None, None),
            P("segment", None, None, None),
            P("segment", None, None, None),
            P("segment", None, None, None),
            P("segment", None, None),
            P("segment", "dom", None),
            P("segment", "dom"),
            P("segment", "dom", None, None, None),
        ),
        out_specs=P("segment", "dom", None),
        check_vma=False,
    )
```

```python
import functools

import jax
import jax.numpy as jnp
from jax import lax
from jax.experimental import pallas as pl
from jax.experimental.pallas import tpu as pltpu
from jax.sharding import PartitionSpec as P

D = 512
BLK = 128
BD = 4
K = 6
SEG = 4
Y, Z = 4, 8
HALF = D // 2
META = 16
ROWS = 2 * K * BLK
BF = jnp.bfloat16
F32 = jnp.float32
ANY = pl.BlockSpec(memory_space=pl.ANY)
HBM = pl.BlockSpec(memory_space=pltpu.HBM)
SMEM = pl.BlockSpec(memory_space=pltpu.SMEM)
VMEM = pl.BlockSpec(memory_space=pltpu.VMEM)


def silu(v):
    return (0.5 * v) * (1.0 + jnp.tanh(0.5 * v))


def params(mib):
    return pltpu.CompilerParams(vmem_limit_bytes=mib * 2**20)


def by_segment(x):
    return [(i, i ^ x) for i in range(SEG)]


def dom_pairs(move):
    out = []
    for d in range(Z * Y * 2):
        z, y, c = move(d // (2 * Y), d // 2 % Y, d % 2)
        out.append((d, ((z % Z) * Y + y % Y) * 2 + c % 2))
    return out


def by_y(x):
    return dom_pairs(lambda z, y, c: (z, y ^ x, c))


Z_FAR = dom_pairs(lambda z, y, c: (z ^ 2, y, c))
Z_EVEN = dom_pairs(lambda z, y, c: (z ^ 1, y, c))
Z_ODD = dom_pairs(lambda z, y, c: (((z + 1) ^ 1) - 1, y, c))
OTHER_CORE = dom_pairs(lambda z, y, c: (z, y, c ^ 1))
NEXT_CHIP = [(d, (((d + 1) ^ 1) - 1) % (2 * Y * Z)) for d in range(2 * Y * Z)]


def place():
    p, dom = lax.axis_index("segment"), lax.axis_index("dom")
    return p, dom, (dom >> 1) & 3, (dom >> 3) & 1, dom & 1


def sender_rows(rows, w):
    return silu(jnp.dot(rows, w, preferred_element_type=F32)).astype(BF)


def halo_places():
    core = place()[4]
    return pl.multiple_of((1 - core) * (5 * BLK), BLK), pl.multiple_of(core * (5 * BLK), BLK)


def gather(tile, code, sbuf, gbuf):
    for b in range(BD):
        slots = range(b * K, (b + 1) * K)
        places = [pl.multiple_of(code(i) * BLK, BLK) for i in slots]
        got = jnp.dot(
            jnp.concatenate([tile(i) for i in slots], axis=1),
            jnp.concatenate([sbuf[pl.ds(at, BLK), :] for at in places], axis=0),
            preferred_element_type=F32,
        )
        gbuf[b * BLK : (b + 1) * BLK, :] = got.astype(BF)


def update_rows(h, gathered, w, gain):
    mixed = jnp.dot(h, w[1], preferred_element_type=F32)
    mixed = mixed + jnp.dot(gathered, w[2], preferred_element_type=F32)
    mean = jnp.mean(mixed * mixed, axis=-1, keepdims=True)
    update = silu(mixed * lax.rsqrt(mean + 1e-05) * gain).astype(BF)
    return (h.astype(F32) + jnp.dot(update, w[3], preferred_element_type=F32)).astype(BF)


def own_small(src, cnt, gain):
    dom = place()[1]
    row = lax.broadcasted_iota(jnp.int32, (META, BLK), 0)
    col = lax.broadcasted_iota(jnp.int32, (META, BLK), 1)
    meta = jnp.zeros((META, BLK), F32)
    for i in range(BD * K):
        used, code = own_slot(src, cnt, dom, i)
        meta = jnp.where((row == 0) & (col == i), jnp.where(used, code, 7).astype(F32), meta)
    left = gain[0]
    for part in range(3):
        piece = left.astype(BF).astype(F32)
        left = left - piece
        for i in range(4):
            meta = jnp.where(row == 1 + 4 * part + i, piece[:, i * BLK : (i + 1) * BLK], meta)
    return meta.astype(BF)


def own_slot(src, cnt, dom, i):
    b, k = divmod(i, K)
    return k < cnt[0, b], (src[0, b, k] - (dom * BD - 1) + 512) & 255


def first_kernel(order, src, cnt, gain, inner, outer, samples, w0, w1, w2, w3, tiles, *rest):
    outs, (wbuf, tbuf, sbuf, gbuf, hbuf, ibuf, obuf, wsem, tsem, hsem, esem) = rest[:-11], rest[-11:]
    p, dom, _, _, _ = place()

    @pl.when(p == 0)
    def _():
        for m, w in enumerate((w0, w1, w2, w3)):
            pltpu.make_async_copy(w.at[0, 0], wbuf.at[m], wsem.at[m]).start()
        for n, sample in enumerate(order):
            pltpu.make_async_copy(samples.at[sample], hbuf.at[n], hsem.at[n]).start()
            pltpu.make_async_copy(inner.at[sample], ibuf.at[n], esem.at[0, n]).start()
            pltpu.make_async_copy(outer.at[sample], obuf.at[n], esem.at[1, n]).start()
        pltpu.make_async_copy(tiles.at[0], tbuf, tsem).start()
        in_place = halo_places()

        def tile(i):
            b, k = divmod(i, K)
            used, _ = own_slot(src, cnt, dom, i)
            t = tbuf[b, k]
            return jnp.where(used, t, jnp.zeros_like(t))

        def code(i):
            used, at = own_slot(src, cnt, dom, i)
            return jnp.where(used, at, 0)

        for n, sample in enumerate(order):
            if n == 0:
                pltpu.make_async_copy(w0.at[0, 0], wbuf.at[0], wsem.at[0]).wait()
            pltpu.make_async_copy(samples.at[sample], hbuf.at[n], hsem.at[n]).wait()
            pltpu.make_async_copy(inner.at[sample], ibuf.at[n], esem.at[0, n]).wait()
            pltpu.make_async_copy(outer.at[sample], obuf.at[n], esem.at[1, n]).wait()
            for at, block in zip(in_place, (ibuf, obuf)):
                sbuf[pl.ds(at, BLK), :] = sender_rows(block[n], wbuf[0])
            for i in range(2):
                rows = slice(i * HALF, (i + 1) * HALF)
                sbuf[BLK + i * HALF : BLK + (i + 1) * HALF, :] = sender_rows(hbuf[n, rows, :], wbuf[0])
            if n == 0:
                pltpu.make_async_copy(tiles.at[0], tbuf, tsem).wait()
                for m, w in ((1, w1), (2, w2), (3, w3)):
                    pltpu.make_async_copy(w.at[0, 0], wbuf.at[m], wsem.at[m]).wait()
            gather(tile, code, sbuf, gbuf)
            for i in range(2):
                rows = slice(i * HALF, (i + 1) * HALF)
                new = update_rows(hbuf[n, rows, :], gbuf[rows, :], wbuf, gain[0])
                if sample == 0:
                    outs[0][rows, :] = new
                    continue
                for j in range(4):
                    which, at = layout(sample, j)
                    outs[which][at + i * HALF : at + (i + 1) * HALF, :] = new[:, j * BLK : (j + 1) * BLK]

    if 0 not in order:

        @pl.when(p != 0)
        def _():
            moves = [
                pltpu.make_async_copy(
                    tiles.at[0, b, k], out.at[pl.ds((b * K + k) * BLK, BLK)], wsem.at[n]
                )
                for n, out in enumerate(outs)
                for b in range(BD)
                for k in range(K)
            ]
            for m in moves:
                m.start()
            small = own_small(src, cnt, gain)
            for n, out in enumerate(outs):
                out[2 * ROWS :, :] = small
                there = out.at[pl.ds(0, 2 * ROWS)]
                pltpu.make_async_copy(there, there, wsem.at[n]).wait()


def layout(sample, j):
    if sample == 1:
        return 0, 2 * D + j * D
    if sample == 3:
        return 1, j * D
    return (0, j * D) if j < 2 else (1, 4 * D + (j - 2) * D)


def first_call(order, src, cnt, gain, inner, outer, samples, ws, tiles):
    n = len(order)
    shape = (D, D) if 0 in order else (2 * ROWS + META, BLK)
    return pl.pallas_call(
        functools.partial(first_kernel, order),
        out_shape=[jax.ShapeDtypeStruct(shape, BF)] * (1 if 0 in order else 2),
        in_specs=[SMEM, SMEM, VMEM] + [ANY] * 8,
        out_specs=[VMEM] * (1 if 0 in order else 2),
        scratch_shapes=[
            pltpu.VMEM((4, D, D), BF),
            pltpu.VMEM((BD, K, BLK, BLK), BF),
            pltpu.VMEM(((BD + 2) * BLK, D), BF),
            pltpu.VMEM((BD * BLK, D), BF),
            pltpu.VMEM((n, D, D), BF),
            pltpu.VMEM((n, BLK, D), BF),
            pltpu.VMEM((n, BLK, D), BF),
            pltpu.SemaphoreType.DMA((4,)),
            pltpu.SemaphoreType.DMA,
            pltpu.SemaphoreType.DMA((n,)),
            pltpu.SemaphoreType.DMA((2, n)),
        ],
        compiler_params=params(20 if 0 in order else 60),
        cost_estimate=pl.CostEstimate(
            flops=2_000_000_000 * n, bytes_accessed=4_000_000, transcendentals=262144 * n
        ),
        name=f"first{n}",
    )(src, cnt, gain, inner, outer, samples, *ws, tiles)


def arrived_kernel(h0, near, far, mixed_a, mixed_b, out, sem):
    p = lax.axis_index("segment")

    @pl.when(p == 0)
    def _():
        pltpu.make_async_copy(h0, out, sem).start()

    for q in (1, 2, 3):

        @pl.when(p == q)
        def _():
            for j in range(4):
                which, at = layout(q, j)
                src = (near, far)[which]
                if q == 2:
                    src, at = (mixed_a, at) if which == 0 else (mixed_b, at - ROWS)
                pltpu.make_async_copy(
                    src.at[pl.ds(at, D)], out.at[:, pl.ds(j * BLK, BLK)], sem
                ).start()

    pltpu.make_async_copy(h0, out, sem).wait()


def arrived_call(*args):
    return pl.pallas_call(
        arrived_kernel,
        out_shape=jax.ShapeDtypeStruct((D, D), BF),
        in_specs=[ANY] * 5,
        out_specs=VMEM,
        scratch_shapes=[pltpu.SemaphoreType.DMA],
        compiler_params=params(4),
        name="arrived",
    )(*args)


def copies(kernel_name, plan, shapes, *args, mib=4):
    def kernel(*refs):
        ins, outs, sem = refs[: len(args)], refs[len(args) : -1], refs[-1]
        moves = [
            pltpu.make_async_copy(a, b, sem.at[i]) for i, (a, b) in enumerate(plan(ins, outs))
        ]
        for m in moves:
            m.start()
        for m in moves:
            m.wait()

    return pl.pallas_call(
        kernel,
        out_shape=[jax.ShapeDtypeStruct(shape, BF) for shape in shapes],
        in_specs=[ANY] * len(args),
        out_specs=[ANY] * len(shapes),
        scratch_shapes=[pltpu.SemaphoreType.DMA((4,))],
        compiler_params=params(mib),
        cost_estimate=pl.CostEstimate(flops=0, bytes_accessed=2_000_000, transcendentals=0),
        name=kernel_name,
    )(*args)


def edges(samples):
    def plan(ins, outs):
        core = place()[4]
        last = 3 * BLK
        return [
            (ins[0].at[:, pl.ds(pl.multiple_of((1 - core) * last, BLK), BLK)], outs[0]),
            (ins[0].at[:, pl.ds(pl.multiple_of(core * last, BLK), BLK)], outs[1]),
        ]

    return copies("edges", plan, [(4, BLK, D)] * 2, samples, mib=60)


def joined(ring):
    def plan(ins, outs):
        return [(ins[r], outs[0].at[r]) for r in range(4)]

    return copies("joined", plan, [(4, D, HALF)], *ring)[0]


STAGE_BY_Y = {1: True, 2: True, 3: False}


def weights_kernel(section, *refs):
    own, stage = refs[:4], refs[4:6]
    out, sem = refs[-2:]
    p, dom, y, _, c = place()

    @pl.when(p == section)
    def _():
        for m in range(4):
            pltpu.make_async_copy(own[m].at[0, 0], out.at[m], sem.at[m]).start()

    @pl.when(p != section)
    def _():
        first = y if STAGE_BY_Y[section] else (dom >> 3) & 3
        for m in range(4):
            for core in range(2):
                cols = pl.multiple_of((c ^ core) * HALF, HALF)
                pltpu.make_async_copy(
                    stage[core].at[first ^ m], out.at[m, :, pl.ds(cols, HALF)], sem.at[m]
                ).start()

    for m in range(4):
        pltpu.make_async_copy(own[m].at[0, 0], out.at[m], sem.at[m]).wait()


def weights_call(section, own, stage):
    return pl.pallas_call(
        functools.partial(weights_kernel, section),
        out_shape=jax.ShapeDtypeStruct((4, D, D), BF),
        in_specs=[ANY] * 6,
        out_specs=VMEM,
        scratch_shapes=[pltpu.SemaphoreType.DMA((4,))],
        compiler_params=params(4),
        cost_estimate=pl.CostEstimate(flops=0, bytes_accessed=4_000_000, transcendentals=0),
        name=f"weights{section}",
    )(*own, *stage)


def tiles_kernel(section, own, near, far, mixed_a, mixed_b, tiles, codes, gain, meta, sem):
    for q in range(SEG):

        @pl.when(lax.axis_index("segment") == q)
        def _():
            x = q ^ section
            if x == 2:
                first, second, small = mixed_a, mixed_b, mixed_b.at[pl.ds(ROWS, META)]
            else:
                whole = {0: own, 1: near, 3: far}[x]
                first, second = whole, whole.at[pl.ds(ROWS, ROWS)]
                small = whole.at[pl.ds(2 * ROWS, META)]
            for i in range(2 * K):
                rows = pl.ds(i * BLK, BLK)
                pltpu.make_async_copy(first.at[rows], tiles.at[i], sem.at[0]).start()
                pltpu.make_async_copy(second.at[rows], tiles.at[2 * K + i], sem.at[1]).start()
            pltpu.make_async_copy(small, meta, sem.at[2]).start()

    pltpu.make_async_copy(own.at[pl.ds(2 * ROWS, META)], meta, sem.at[2]).wait()
    for half in range(2):
        there = tiles.at[pl.ds(half * 2 * K, 2 * K)]
        pltpu.make_async_copy(there, there, sem.at[half]).wait()
    m = meta[...].astype(F32)
    code = m[:8]
    codes[...] = jnp.where(code < 7.0, code, 0.0).astype(jnp.int32)
    gain[...] = jnp.concatenate(
        [m[1 + i : 2 + i] + (m[5 + i : 6 + i] + m[9 + i : 10 + i]) for i in range(4)], axis=1
    )
    for i in range(BD * K):
        used = jnp.broadcast_to(m[0:1, i : i + 1], (BLK, BLK)) < 7.0
        tiles[i] = jnp.where(used, tiles[i].astype(F32), 0.0).astype(BF)


def tiles_call(section, arrays):
    return pl.pallas_call(
        functools.partial(tiles_kernel, section),
        out_shape=[
            jax.ShapeDtypeStruct((BD * K, BLK, BLK), BF),
            jax.ShapeDtypeStruct((8, BLK), jnp.int32),
            jax.ShapeDtypeStruct((1, D), F32),
        ],
        in_specs=[ANY] * len(arrays),
        out_specs=[VMEM] * 3,
        scratch_shapes=[pltpu.VMEM((META, BLK), BF), pltpu.SemaphoreType.DMA((3,))],
        compiler_params=params(4),
        cost_estimate=pl.CostEstimate(flops=0, bytes_accessed=2_000_000, transcendentals=0),
        name=f"tiles{section}",
    )(*arrays)


def section_kernel(codes, gain, tiles, w, h, inner, outer, sender, out, sbuf, gbuf):
    sbuf[BLK : 5 * BLK, :] = sender[...]
    for at, block in zip(halo_places(), (inner, outer)):
        sbuf[pl.ds(at, BLK), :] = block[...]
    gather(lambda i: tiles[i], lambda i: codes[0, i], sbuf, gbuf)
    for i in range(2):
        rows = slice(i * HALF, (i + 1) * HALF)
        out[rows, :] = update_rows(h[rows, :], gbuf[rows, :], w, gain[...])


def section_call(section, codes, gain, tiles, w, h, inner, outer, sender):
    return pl.pallas_call(
        section_kernel,
        out_shape=jax.ShapeDtypeStruct((BD * BLK, D), BF),
        in_specs=[SMEM] + [VMEM] * 7,
        out_specs=VMEM,
        scratch_shapes=[
            pltpu.VMEM(((BD + 2) * BLK, D), BF),
            pltpu.VMEM((BD * BLK, D), BF),
        ],
        compiler_params=params(16),
        cost_estimate=pl.CostEstimate(
            flops=1_500_000_000, bytes_accessed=4_000_000, transcendentals=262144
        ),
        name=f"section{section}",
    )(codes, gain, tiles, w, h, inner, outer, sender)


def sender_kernel(h, w, full, inner, outer):
    core = place()[4]
    for i in range(2):
        rows = slice(i * HALF, (i + 1) * HALF)
        full[rows, :] = sender_rows(h[rows, :], w[0])
    inner[...] = full[pl.ds(pl.multiple_of((1 - core) * 3 * BLK, BLK), BLK), :]
    outer[...] = full[pl.ds(pl.multiple_of(core * 3 * BLK, BLK), BLK), :]


def sender_call(section, h, w):
    return pl.pallas_call(
        sender_kernel,
        out_shape=[
            jax.ShapeDtypeStruct((BD * BLK, D), BF),
            jax.ShapeDtypeStruct((BLK, D), BF),
            jax.ShapeDtypeStruct((BLK, D), BF),
        ],
        in_specs=[VMEM, VMEM],
        out_specs=[VMEM] * 3,
        compiler_params=params(8),
        cost_estimate=pl.CostEstimate(
            flops=270_000_000, bytes_accessed=1_500_000, transcendentals=262144
        ),
        name=f"sender{section}",
    )(h, w)


def after(values, *others):
    return lax.optimization_barrier((values, others))[0]


def over_segments(value, x):
    return lax.ppermute(value, "segment", by_segment(x))


def over_dom(value, pairs):
    return lax.ppermute(value, "dom", pairs)


def exchange(inner, outer):
    return over_dom(inner, OTHER_CORE), over_dom(outer, NEXT_CHIP)


def shards(samples, w_source, w_self, w_message, w_output, norm_gain, tile_source, tile_count, tile_value):
    p, dom, y, _, core = place()
    ws = [w_source, w_self, w_message, w_output]
    edge = edges(samples)
    inner, outer = exchange(*edge)

    m = jnp.where(p == 3, (dom >> 3) & 3, y)
    a, b, c, d = (lax.dynamic_slice(w[0, 0], (0, core * HALF), (D, HALF)) for w in ws)
    piece = jnp.where(m < 2, jnp.where(m == 0, a, b), jnp.where(m == 2, c, d))
    piece = after(piece, edge)
    x1, x3, x2 = over_segments(piece, 1), over_segments(piece, 3), over_segments(piece, 2)

    small = (tile_source, tile_count, norm_gain, inner, outer, samples, ws, tile_value)
    own, own_far = first_call((2, 1, 3), *small)
    near, far = over_segments(own, 1), over_segments(own_far, 3)
    (h0,) = first_call((0,), *small)
    mixed_b, mixed_a = over_segments(far[ROWS:], 1), over_segments(near[:ROWS], 3)
    arrays = [own, near, far, mixed_a, mixed_b]

    def ring(own, routes):
        return [own] + [over_dom(own, route) for route in routes]

    def both(pieces):
        return pieces, over_dom(pieces, OTHER_CORE)

    over_y, over_z = [by_y(x) for x in (1, 2, 3)], [Z_EVEN, Z_FAR, Z_ODD]
    x1, x2, x3 = after((x1, x2, x3), own, own_far)
    ring1 = ring(jnp.where(p == 2, x3, jnp.where(p == 3, x2, x1)), over_y)
    then = jnp.where(p == 0, x2, jnp.where(p == 1, x3, x1))
    last = jnp.where(p == 0, x3, jnp.where(p == 1, x2, x1))
    ring2 = ring(after(then, ring1), over_y)
    stages = {1: both(joined(ring1)), 2: both(joined(ring2))}
    ring3 = ring(after(last, near, far, stages[2]), over_z)
    h = arrived_call(h0, near, far, after(mixed_a, stages[2][0]), mixed_b)
    for section in range(1, SEG):
        w = weights_call(section, ws, stages[section])
        tiles, codes, gain = tiles_call(section, arrays)
        sender, inner, outer = sender_call(section, h, w)
        inner, outer = exchange(inner, outer)
        h = section_call(section, codes, gain, tiles, w, h, inner, outer, sender)
        if section == 1:
            stages[3] = both(joined(after(ring3, h)))
    return h[None]


def solution(mesh):
    return jax.shard_map(
        shards,
        mesh=mesh,
        in_specs=(
            P(None, "dom", None),
            P("segment", None, None, None),
            P("segment", None, None, None),
            P("segment", None, None, None),
            P("segment", None, None, None),
            P("segment", None, None),
            P("segment", "dom", None),
            P("segment", "dom"),
            P("segment", "dom", None, None, None),
        ),
        out_specs=P("segment", "dom", None),
        check_vma=False,
    )
```

```python
import functools

import jax
import jax.numpy as jnp
from jax import lax
from jax.experimental import pallas as pl
from jax.experimental.pallas import tpu as pltpu
from jax.sharding import PartitionSpec as P

D = 512
BLK = 128
BD = 4
K = 6
SEG = 4
Y, Z = 4, 8
HALF = D // 2
META = 16
ROWS = 2 * K * BLK
BF = jnp.bfloat16
F32 = jnp.float32
ANY = pl.BlockSpec(memory_space=pl.ANY)
HBM = pl.BlockSpec(memory_space=pltpu.HBM)
SMEM = pl.BlockSpec(memory_space=pltpu.SMEM)
VMEM = pl.BlockSpec(memory_space=pltpu.VMEM)


def silu(v):
    return (0.5 * v) * (1.0 + jnp.tanh(0.5 * v))


def params(mib):
    return pltpu.CompilerParams(vmem_limit_bytes=mib * 2**20)


def by_segment(x):
    return [(i, i ^ x) for i in range(SEG)]


def dom_pairs(move):
    out = []
    for d in range(Z * Y * 2):
        z, y, c = move(d // (2 * Y), d // 2 % Y, d % 2)
        out.append((d, ((z % Z) * Y + y % Y) * 2 + c % 2))
    return out


def by_y(x):
    return dom_pairs(lambda z, y, c: (z, y ^ x, c))


Z_FAR = dom_pairs(lambda z, y, c: (z ^ 2, y, c))
Z_EVEN = dom_pairs(lambda z, y, c: (z ^ 1, y, c))
Z_ODD = dom_pairs(lambda z, y, c: (((z + 1) ^ 1) - 1, y, c))
OTHER_CORE = dom_pairs(lambda z, y, c: (z, y, c ^ 1))
NEXT_CHIP = [(d, (((d + 1) ^ 1) - 1) % (2 * Y * Z)) for d in range(2 * Y * Z)]


def place():
    p, dom = lax.axis_index("segment"), lax.axis_index("dom")
    return p, dom, (dom >> 1) & 3, (dom >> 3) & 1, dom & 1


def sender_rows(rows, w):
    return silu(jnp.dot(rows, w, preferred_element_type=F32)).astype(BF)


def halo_places():
    core = place()[4]
    return pl.multiple_of((1 - core) * (5 * BLK), BLK), pl.multiple_of(core * (5 * BLK), BLK)


def gather(tile, code, sbuf, gbuf):
    for b in range(BD):
        slots = range(b * K, (b + 1) * K)
        places = [pl.multiple_of(code(i) * BLK, BLK) for i in slots]
        got = jnp.dot(
            jnp.concatenate([tile(i) for i in slots], axis=1),
            jnp.concatenate([sbuf[pl.ds(at, BLK), :] for at in places], axis=0),
            preferred_element_type=F32,
        )
        gbuf[b * BLK : (b + 1) * BLK, :] = got.astype(BF)


def update_rows(h, gathered, w, gain):
    mixed = jnp.dot(h, w[1], preferred_element_type=F32)
    mixed = mixed + jnp.dot(gathered, w[2], preferred_element_type=F32)
    mean = jnp.mean(mixed * mixed, axis=-1, keepdims=True)
    update = silu(mixed * lax.rsqrt(mean + 1e-05) * gain).astype(BF)
    return (h.astype(F32) + jnp.dot(update, w[3], preferred_element_type=F32)).astype(BF)


def own_small(src, cnt, gain):
    dom = place()[1]
    row = lax.broadcasted_iota(jnp.int32, (META, BLK), 0)
    col = lax.broadcasted_iota(jnp.int32, (META, BLK), 1)
    meta = jnp.zeros((META, BLK), F32)
    for i in range(BD * K):
        used, code = own_slot(src, cnt, dom, i)
        meta = jnp.where((row == 0) & (col == i), jnp.where(used, code, 7).astype(F32), meta)
    left = gain[0]
    for part in range(3):
        piece = left.astype(BF).astype(F32)
        left = left - piece
        for i in range(4):
            meta = jnp.where(row == 1 + 4 * part + i, piece[:, i * BLK : (i + 1) * BLK], meta)
    return meta.astype(BF)


def own_slot(src, cnt, dom, i):
    b, k = divmod(i, K)
    return k < cnt[0, b], (src[0, b, k] - (dom * BD - 1) + 512) & 255


def first_kernel(order, src, cnt, gain, inner, outer, samples, w0, w1, w2, w3, tiles, *rest):
    outs, (wbuf, tbuf, sbuf, gbuf, hbuf, ibuf, obuf, wsem, tsem, hsem, esem) = rest[:-11], rest[-11:]
    p, dom, _, _, _ = place()

    @pl.when(p == 0)
    def _():
        for m, w in enumerate((w0, w1, w2, w3)):
            pltpu.make_async_copy(w.at[0, 0], wbuf.at[m], wsem.at[m]).start()
        for n, sample in enumerate(order):
            pltpu.make_async_copy(samples.at[sample], hbuf.at[n], hsem.at[n]).start()
            pltpu.make_async_copy(inner.at[sample], ibuf.at[n], esem.at[0, n]).start()
            pltpu.make_async_copy(outer.at[sample], obuf.at[n], esem.at[1, n]).start()
        pltpu.make_async_copy(tiles.at[0], tbuf, tsem).start()
        in_place = halo_places()

        def tile(i):
            b, k = divmod(i, K)
            used, _ = own_slot(src, cnt, dom, i)
            t = tbuf[b, k]
            return jnp.where(used, t, jnp.zeros_like(t))

        def code(i):
            used, at = own_slot(src, cnt, dom, i)
            return jnp.where(used, at, 0)

        for n, sample in enumerate(order):
            if n == 0:
                pltpu.make_async_copy(w0.at[0, 0], wbuf.at[0], wsem.at[0]).wait()
            pltpu.make_async_copy(samples.at[sample], hbuf.at[n], hsem.at[n]).wait()
            pltpu.make_async_copy(inner.at[sample], ibuf.at[n], esem.at[0, n]).wait()
            pltpu.make_async_copy(outer.at[sample], obuf.at[n], esem.at[1, n]).wait()
            for at, block in zip(in_place, (ibuf, obuf)):
                sbuf[pl.ds(at, BLK), :] = sender_rows(block[n], wbuf[0])
            for i in range(2):
                rows = slice(i * HALF, (i + 1) * HALF)
                sbuf[BLK + i * HALF : BLK + (i + 1) * HALF, :] = sender_rows(hbuf[n, rows, :], wbuf[0])
            if n == 0:
                pltpu.make_async_copy(tiles.at[0], tbuf, tsem).wait()
                for m, w in ((1, w1), (2, w2), (3, w3)):
                    pltpu.make_async_copy(w.at[0, 0], wbuf.at[m], wsem.at[m]).wait()
            gather(tile, code, sbuf, gbuf)
            for i in range(2):
                rows = slice(i * HALF, (i + 1) * HALF)
                new = update_rows(hbuf[n, rows, :], gbuf[rows, :], wbuf, gain[0])
                if sample == 0:
                    outs[0][rows, :] = new
                    continue
                for j in range(4):
                    which, at = layout(sample, j)
                    outs[which][at + i * HALF : at + (i + 1) * HALF, :] = new[:, j * BLK : (j + 1) * BLK]

    if 0 not in order:

        @pl.when(p != 0)
        def _():
            moves = [
                pltpu.make_async_copy(
                    tiles.at[0, b, k], out.at[pl.ds((b * K + k) * BLK, BLK)], wsem.at[n]
                )
                for n, out in enumerate(outs)
                for b in range(BD)
                for k in range(K)
            ]
            for m in moves:
                m.start()
            small = own_small(src, cnt, gain)
            for n, out in enumerate(outs):
                out[2 * ROWS :, :] = small
                there = out.at[pl.ds(0, 2 * ROWS)]
                pltpu.make_async_copy(there, there, wsem.at[n]).wait()


def layout(sample, j):
    if sample == 1:
        return 0, 2 * D + j * D
    if sample == 3:
        return 1, j * D
    return (0, j * D) if j < 2 else (1, 4 * D + (j - 2) * D)


def first_call(order, src, cnt, gain, inner, outer, samples, ws, tiles):
    n = len(order)
    shape = (D, D) if 0 in order else (2 * ROWS + META, BLK)
    return pl.pallas_call(
        functools.partial(first_kernel, order),
        out_shape=[jax.ShapeDtypeStruct(shape, BF)] * (1 if 0 in order else 2),
        in_specs=[SMEM, SMEM, VMEM] + [ANY] * 8,
        out_specs=[VMEM] * (1 if 0 in order else 2),
        scratch_shapes=[
            pltpu.VMEM((4, D, D), BF),
            pltpu.VMEM((BD, K, BLK, BLK), BF),
            pltpu.VMEM(((BD + 2) * BLK, D), BF),
            pltpu.VMEM((BD * BLK, D), BF),
            pltpu.VMEM((n, D, D), BF),
            pltpu.VMEM((n, BLK, D), BF),
            pltpu.VMEM((n, BLK, D), BF),
            pltpu.SemaphoreType.DMA((4,)),
            pltpu.SemaphoreType.DMA,
            pltpu.SemaphoreType.DMA((n,)),
            pltpu.SemaphoreType.DMA((2, n)),
        ],
        compiler_params=params(20 if 0 in order else 60),
        cost_estimate=pl.CostEstimate(
            flops=2_000_000_000 * n, bytes_accessed=4_000_000, transcendentals=262144 * n
        ),
        name=f"first{n}",
    )(src, cnt, gain, inner, outer, samples, *ws, tiles)


def arrived_kernel(h0, near, far, mixed_a, mixed_b, out, sem):
    p = lax.axis_index("segment")

    @pl.when(p == 0)
    def _():
        pltpu.make_async_copy(h0, out, sem).start()

    for q in (1, 2, 3):

        @pl.when(p == q)
        def _():
            for j in range(4):
                which, at = layout(q, j)
                src = (near, far)[which]
                if q == 2:
                    src, at = (mixed_a, at) if which == 0 else (mixed_b, at - ROWS)
                pltpu.make_async_copy(
                    src.at[pl.ds(at, D)], out.at[:, pl.ds(j * BLK, BLK)], sem
                ).start()

    pltpu.make_async_copy(h0, out, sem).wait()


def arrived_call(*args):
    return pl.pallas_call(
        arrived_kernel,
        out_shape=jax.ShapeDtypeStruct((D, D), BF),
        in_specs=[ANY] * 5,
        out_specs=VMEM,
        scratch_shapes=[pltpu.SemaphoreType.DMA],
        compiler_params=params(4),
        name="arrived",
    )(*args)


def copies(kernel_name, plan, shapes, *args, mib=4, out=ANY):
    def kernel(*refs):
        ins, outs, sem = refs[: len(args)], refs[len(args) : -1], refs[-1]
        moves = [
            pltpu.make_async_copy(a, b, sem.at[i]) for i, (a, b) in enumerate(plan(ins, outs))
        ]
        for m in moves:
            m.start()
        for m in moves:
            m.wait()

    return pl.pallas_call(
        kernel,
        out_shape=[jax.ShapeDtypeStruct(shape, BF) for shape in shapes],
        in_specs=[ANY] * len(args),
        out_specs=[out] * len(shapes),
        scratch_shapes=[pltpu.SemaphoreType.DMA((4,))],
        compiler_params=params(mib),
        cost_estimate=pl.CostEstimate(flops=0, bytes_accessed=2_000_000, transcendentals=0),
        name=kernel_name,
    )(*args)


def edges(samples):
    def plan(ins, outs):
        core = place()[4]
        last = 3 * BLK
        return [
            (ins[0].at[:, pl.ds(pl.multiple_of((1 - core) * last, BLK), BLK)], outs[0]),
            (ins[0].at[:, pl.ds(pl.multiple_of(core * last, BLK), BLK)], outs[1]),
        ]

    return copies("edges", plan, [(4, BLK, D)] * 2, samples, mib=60, out=VMEM)


def joined(ring):
    def plan(ins, outs):
        return [(ins[r], outs[0].at[r]) for r in range(4)]

    return copies("joined", plan, [(4, D, HALF)], *ring)[0]


STAGE_BY_Y = {1: True, 2: True, 3: False}


def weights_kernel(section, *refs):
    own, stage = refs[:4], refs[4:6]
    out, sem = refs[-2:]
    p, dom, y, _, c = place()

    @pl.when(p == section)
    def _():
        for m in range(4):
            pltpu.make_async_copy(own[m].at[0, 0], out.at[m], sem.at[m]).start()

    @pl.when(p != section)
    def _():
        first = y if STAGE_BY_Y[section] else (dom >> 3) & 3
        for m in range(4):
            for core in range(2):
                cols = pl.multiple_of((c ^ core) * HALF, HALF)
                pltpu.make_async_copy(
                    stage[core].at[first ^ m], out.at[m, :, pl.ds(cols, HALF)], sem.at[m]
                ).start()

    for m in range(4):
        pltpu.make_async_copy(own[m].at[0, 0], out.at[m], sem.at[m]).wait()


def weights_call(section, own, stage):
    return pl.pallas_call(
        functools.partial(weights_kernel, section),
        out_shape=jax.ShapeDtypeStruct((4, D, D), BF),
        in_specs=[ANY] * 6,
        out_specs=VMEM,
        scratch_shapes=[pltpu.SemaphoreType.DMA((4,))],
        compiler_params=params(4),
        cost_estimate=pl.CostEstimate(flops=0, bytes_accessed=4_000_000, transcendentals=0),
        name=f"weights{section}",
    )(*own, *stage)


def tiles_kernel(section, own, near, far, mixed_a, mixed_b, tiles, codes, gain, meta, sem):
    for q in range(SEG):

        @pl.when(lax.axis_index("segment") == q)
        def _():
            x = q ^ section
            if x == 2:
                first, second, small = mixed_a, mixed_b, mixed_b.at[pl.ds(ROWS, META)]
            else:
                whole = {0: own, 1: near, 3: far}[x]
                first, second = whole, whole.at[pl.ds(ROWS, ROWS)]
                small = whole.at[pl.ds(2 * ROWS, META)]
            for i in range(2 * K):
                rows = pl.ds(i * BLK, BLK)
                pltpu.make_async_copy(first.at[rows], tiles.at[i], sem.at[0]).start()
                pltpu.make_async_copy(second.at[rows], tiles.at[2 * K + i], sem.at[1]).start()
            pltpu.make_async_copy(small, meta, sem.at[2]).start()

    pltpu.make_async_copy(own.at[pl.ds(2 * ROWS, META)], meta, sem.at[2]).wait()
    for half in range(2):
        there = tiles.at[pl.ds(half * 2 * K, 2 * K)]
        pltpu.make_async_copy(there, there, sem.at[half]).wait()
    m = meta[...].astype(F32)
    code = m[:8]
    codes[...] = jnp.where(code < 7.0, code, 0.0).astype(jnp.int32)
    gain[...] = jnp.concatenate(
        [m[1 + i : 2 + i] + (m[5 + i : 6 + i] + m[9 + i : 10 + i]) for i in range(4)], axis=1
    )
    for i in range(BD * K):
        used = jnp.broadcast_to(m[0:1, i : i + 1], (BLK, BLK)) < 7.0
        tiles[i] = jnp.where(used, tiles[i].astype(F32), 0.0).astype(BF)


def tiles_call(section, arrays):
    return pl.pallas_call(
        functools.partial(tiles_kernel, section),
        out_shape=[
            jax.ShapeDtypeStruct((BD * K, BLK, BLK), BF),
            jax.ShapeDtypeStruct((8, BLK), jnp.int32),
            jax.ShapeDtypeStruct((1, D), F32),
        ],
        in_specs=[ANY] * len(arrays),
        out_specs=[VMEM] * 3,
        scratch_shapes=[pltpu.VMEM((META, BLK), BF), pltpu.SemaphoreType.DMA((3,))],
        compiler_params=params(4),
        cost_estimate=pl.CostEstimate(flops=0, bytes_accessed=2_000_000, transcendentals=0),
        name=f"tiles{section}",
    )(*arrays)


def section_kernel(codes, gain, tiles, w, h, inner, outer, sender, out, sbuf, gbuf):
    sbuf[BLK : 5 * BLK, :] = sender[...]
    for at, block in zip(halo_places(), (inner, outer)):
        sbuf[pl.ds(at, BLK), :] = block[...]
    gather(lambda i: tiles[i], lambda i: codes[0, i], sbuf, gbuf)
    for i in range(2):
        rows = slice(i * HALF, (i + 1) * HALF)
        out[rows, :] = update_rows(h[rows, :], gbuf[rows, :], w, gain[...])


def section_call(section, codes, gain, tiles, w, h, inner, outer, sender):
    return pl.pallas_call(
        section_kernel,
        out_shape=jax.ShapeDtypeStruct((BD * BLK, D), BF),
        in_specs=[SMEM] + [VMEM] * 7,
        out_specs=VMEM,
        scratch_shapes=[
            pltpu.VMEM(((BD + 2) * BLK, D), BF),
            pltpu.VMEM((BD * BLK, D), BF),
        ],
        compiler_params=params(16),
        cost_estimate=pl.CostEstimate(
            flops=1_500_000_000, bytes_accessed=4_000_000, transcendentals=262144
        ),
        name=f"section{section}",
    )(codes, gain, tiles, w, h, inner, outer, sender)


def sender_kernel(h, w, full, inner, outer):
    core = place()[4]
    for i in range(2):
        rows = slice(i * HALF, (i + 1) * HALF)
        full[rows, :] = sender_rows(h[rows, :], w[0])
    inner[...] = full[pl.ds(pl.multiple_of((1 - core) * 3 * BLK, BLK), BLK), :]
    outer[...] = full[pl.ds(pl.multiple_of(core * 3 * BLK, BLK), BLK), :]


def sender_call(section, h, w):
    return pl.pallas_call(
        sender_kernel,
        out_shape=[
            jax.ShapeDtypeStruct((BD * BLK, D), BF),
            jax.ShapeDtypeStruct((BLK, D), BF),
            jax.ShapeDtypeStruct((BLK, D), BF),
        ],
        in_specs=[VMEM, VMEM],
        out_specs=[VMEM] * 3,
        compiler_params=params(8),
        cost_estimate=pl.CostEstimate(
            flops=270_000_000, bytes_accessed=1_500_000, transcendentals=262144
        ),
        name=f"sender{section}",
    )(h, w)


def after(values, *others):
    return lax.optimization_barrier((values, others))[0]


def over_segments(value, x):
    return lax.ppermute(value, "segment", by_segment(x))


def over_dom(value, pairs):
    return lax.ppermute(value, "dom", pairs)


def exchange(inner, outer):
    return over_dom(inner, OTHER_CORE), over_dom(outer, NEXT_CHIP)


def shards(samples, w_source, w_self, w_message, w_output, norm_gain, tile_source, tile_count, tile_value):
    p, dom, y, _, core = place()
    ws = [w_source, w_self, w_message, w_output]
    edge = edges(samples)
    inner, outer = exchange(*edge)

    m = jnp.where(p == 3, (dom >> 3) & 3, y)
    a, b, c, d = (lax.dynamic_slice(w[0, 0], (0, core * HALF), (D, HALF)) for w in ws)
    piece = jnp.where(m < 2, jnp.where(m == 0, a, b), jnp.where(m == 2, c, d))
    piece = after(piece, edge)
    x1, x3, x2 = over_segments(piece, 1), over_segments(piece, 3), over_segments(piece, 2)

    small = (tile_source, tile_count, norm_gain, inner, outer, samples, ws, tile_value)
    own, own_far = first_call((2, 1, 3), *small)
    near, far = over_segments(own, 1), over_segments(own_far, 3)
    (h0,) = first_call((0,), *small)
    mixed_b, mixed_a = over_segments(far[ROWS:], 1), over_segments(near[:ROWS], 3)
    arrays = [own, near, far, mixed_a, mixed_b]

    def ring(own, routes):
        return [own] + [over_dom(own, route) for route in routes]

    def both(pieces):
        return pieces, over_dom(pieces, OTHER_CORE)

    over_y = [by_y(x) for x in (1, 2, 3)]
    x1, x2, x3 = after((x1, x2, x3), own, own_far)
    ring1 = ring(jnp.where(p == 2, x3, jnp.where(p == 3, x2, x1)), over_y)
    then = jnp.where(p == 0, x2, jnp.where(p == 1, x3, x1))
    last = jnp.where(p == 0, x3, jnp.where(p == 1, x2, x1))
    ring2 = ring(after(then, ring1), over_y)
    stages = {1: both(joined(ring1)), 2: both(joined(ring2))}
    last = after(last, near, far)
    ring3 = [last, over_dom(last, Z_EVEN), None, over_dom(last, Z_ODD)]
    h = arrived_call(h0, near, far, after(mixed_a, stages[2][0]), mixed_b)
    for section in range(1, SEG):
        w = weights_call(section, ws, stages[section])
        tiles, codes, gain = tiles_call(section, arrays)
        sender, inner, outer = sender_call(section, h, w)
        inner, outer = exchange(inner, outer)
        if section == 1:
            ring3[2] = over_dom(after(last, inner, outer), Z_FAR)
        elif section == 2:
            stages[3] = both(joined(after(ring3, inner, outer)))
        h = section_call(section, codes, gain, tiles, w, h, inner, outer, sender)
    return h[None]


def solution(mesh):
    return jax.shard_map(
        shards,
        mesh=mesh,
        in_specs=(
            P(None, "dom", None),
            P("segment", None, None, None),
            P("segment", None, None, None),
            P("segment", None, None, None),
            P("segment", None, None, None),
            P("segment", None, None),
            P("segment", "dom", None),
            P("segment", "dom"),
            P("segment", "dom", None, None, None),
        ),
        out_specs=P("segment", "dom", None),
        check_vma=False,
    )
```

```python
import functools

import jax
import jax.numpy as jnp
from jax import lax
from jax.experimental import pallas as pl
from jax.experimental.pallas import tpu as pltpu
from jax.sharding import PartitionSpec as P

D = 512
BLK = 128
BD = 4
K = 6
SEG = 4
Y, Z = 4, 8
HALF = D // 2
META = 16
ROWS = 2 * K * BLK
BF = jnp.bfloat16
F32 = jnp.float32
ANY = pl.BlockSpec(memory_space=pl.ANY)
HBM = pl.BlockSpec(memory_space=pltpu.HBM)
SMEM = pl.BlockSpec(memory_space=pltpu.SMEM)
VMEM = pl.BlockSpec(memory_space=pltpu.VMEM)


def silu(v):
    return (0.5 * v) * (1.0 + jnp.tanh(0.5 * v))


def params(mib):
    return pltpu.CompilerParams(vmem_limit_bytes=mib * 2**20)


def by_segment(x):
    return [(i, i ^ x) for i in range(SEG)]


def dom_pairs(move):
    out = []
    for d in range(Z * Y * 2):
        z, y, c = move(d // (2 * Y), d // 2 % Y, d % 2)
        out.append((d, ((z % Z) * Y + y % Y) * 2 + c % 2))
    return out


def by_y(x):
    return dom_pairs(lambda z, y, c: (z, y ^ x, c))


Z_FAR = dom_pairs(lambda z, y, c: (z ^ 2, y, c))
Z_EVEN = dom_pairs(lambda z, y, c: (z ^ 1, y, c))
Z_ODD = dom_pairs(lambda z, y, c: (((z + 1) ^ 1) - 1, y, c))
OTHER_CORE = dom_pairs(lambda z, y, c: (z, y, c ^ 1))
NEXT_CHIP = [(d, (((d + 1) ^ 1) - 1) % (2 * Y * Z)) for d in range(2 * Y * Z)]


def place():
    p, dom = lax.axis_index("segment"), lax.axis_index("dom")
    return p, dom, (dom >> 1) & 3, (dom >> 3) & 1, dom & 1


def sender_rows(rows, w):
    return silu(jnp.dot(rows, w, preferred_element_type=F32)).astype(BF)


def halo_places():
    core = place()[4]
    return pl.multiple_of((1 - core) * (5 * BLK), BLK), pl.multiple_of(core * (5 * BLK), BLK)


def gather(tile, code, sbuf, gbuf):
    for b in range(BD):
        slots = range(b * K, (b + 1) * K)
        places = [pl.multiple_of(code(i) * BLK, BLK) for i in slots]
        got = jnp.dot(
            jnp.concatenate([tile(i) for i in slots], axis=1),
            jnp.concatenate([sbuf[pl.ds(at, BLK), :] for at in places], axis=0),
            preferred_element_type=F32,
        )
        gbuf[b * BLK : (b + 1) * BLK, :] = got.astype(BF)


def update_rows(h, gathered, w, gain):
    mixed = jnp.dot(h, w[1], preferred_element_type=F32)
    mixed = mixed + jnp.dot(gathered, w[2], preferred_element_type=F32)
    mean = jnp.mean(mixed * mixed, axis=-1, keepdims=True)
    update = silu(mixed * lax.rsqrt(mean + 1e-05) * gain).astype(BF)
    return (h.astype(F32) + jnp.dot(update, w[3], preferred_element_type=F32)).astype(BF)


def own_small(src, cnt, gain):
    dom = place()[1]
    row = lax.broadcasted_iota(jnp.int32, (META, BLK), 0)
    col = lax.broadcasted_iota(jnp.int32, (META, BLK), 1)
    meta = jnp.zeros((META, BLK), F32)
    for i in range(BD * K):
        used, code = own_slot(src, cnt, dom, i)
        meta = jnp.where((row == 0) & (col == i), jnp.where(used, code, 7).astype(F32), meta)
    left = gain[0]
    for part in range(3):
        piece = left.astype(BF).astype(F32)
        left = left - piece
        for i in range(4):
            meta = jnp.where(row == 1 + 4 * part + i, piece[:, i * BLK : (i + 1) * BLK], meta)
    return meta.astype(BF)


def own_slot(src, cnt, dom, i):
    b, k = divmod(i, K)
    return k < cnt[0, b], (src[0, b, k] - (dom * BD - 1) + 512) & 255


def first_kernel(order, src, cnt, gain, inner, outer, samples, w0, w1, w2, w3, tiles, *rest):
    outs, (wbuf, tbuf, sbuf, gbuf, hbuf, ibuf, obuf, wsem, tsem, hsem, esem) = rest[:-11], rest[-11:]
    p, dom, _, _, _ = place()

    @pl.when(p == 0)
    def _():
        for m, w in enumerate((w0, w1, w2, w3)):
            pltpu.make_async_copy(w.at[0, 0], wbuf.at[m], wsem.at[m]).start()
        for n, sample in enumerate(order):
            pltpu.make_async_copy(samples.at[sample], hbuf.at[n], hsem.at[n]).start()
            pltpu.make_async_copy(inner.at[sample], ibuf.at[n], esem.at[0, n]).start()
            pltpu.make_async_copy(outer.at[sample], obuf.at[n], esem.at[1, n]).start()
        pltpu.make_async_copy(tiles.at[0], tbuf, tsem).start()
        in_place = halo_places()

        def tile(i):
            b, k = divmod(i, K)
            used, _ = own_slot(src, cnt, dom, i)
            t = tbuf[b, k]
            return jnp.where(used, t, jnp.zeros_like(t))

        def code(i):
            used, at = own_slot(src, cnt, dom, i)
            return jnp.where(used, at, 0)

        for n, sample in enumerate(order):
            if n == 0:
                pltpu.make_async_copy(w0.at[0, 0], wbuf.at[0], wsem.at[0]).wait()
            pltpu.make_async_copy(samples.at[sample], hbuf.at[n], hsem.at[n]).wait()
            pltpu.make_async_copy(inner.at[sample], ibuf.at[n], esem.at[0, n]).wait()
            pltpu.make_async_copy(outer.at[sample], obuf.at[n], esem.at[1, n]).wait()
            for at, block in zip(in_place, (ibuf, obuf)):
                sbuf[pl.ds(at, BLK), :] = sender_rows(block[n], wbuf[0])
            for i in range(2):
                rows = slice(i * HALF, (i + 1) * HALF)
                sbuf[BLK + i * HALF : BLK + (i + 1) * HALF, :] = sender_rows(hbuf[n, rows, :], wbuf[0])
            if n == 0:
                pltpu.make_async_copy(tiles.at[0], tbuf, tsem).wait()
                for m, w in ((1, w1), (2, w2), (3, w3)):
                    pltpu.make_async_copy(w.at[0, 0], wbuf.at[m], wsem.at[m]).wait()
            gather(tile, code, sbuf, gbuf)
            for i in range(2):
                rows = slice(i * HALF, (i + 1) * HALF)
                new = update_rows(hbuf[n, rows, :], gbuf[rows, :], wbuf, gain[0])
                if sample == 0:
                    outs[0][rows, :] = new
                    continue
                for j in range(4):
                    which, at = layout(sample, j)
                    outs[which][at + i * HALF : at + (i + 1) * HALF, :] = new[:, j * BLK : (j + 1) * BLK]

    if 0 not in order:

        @pl.when(p != 0)
        def _():
            moves = [
                pltpu.make_async_copy(
                    tiles.at[0, b, k], out.at[pl.ds((b * K + k) * BLK, BLK)], wsem.at[n]
                )
                for n, out in enumerate(outs)
                for b in range(BD)
                for k in range(K)
            ]
            for m in moves:
                m.start()
            small = own_small(src, cnt, gain)
            for n, out in enumerate(outs):
                out[2 * ROWS :, :] = small
                there = out.at[pl.ds(0, 2 * ROWS)]
                pltpu.make_async_copy(there, there, wsem.at[n]).wait()


def layout(sample, j):
    if sample == 1:
        return 0, 2 * D + j * D
    if sample == 3:
        return 1, j * D
    return (0, j * D) if j < 2 else (1, 4 * D + (j - 2) * D)


def first_call(order, src, cnt, gain, inner, outer, samples, ws, tiles):
    n = len(order)
    shape = (D, D) if 0 in order else (2 * ROWS + META, BLK)
    return pl.pallas_call(
        functools.partial(first_kernel, order),
        out_shape=[jax.ShapeDtypeStruct(shape, BF)] * (1 if 0 in order else 2),
        in_specs=[SMEM, SMEM, VMEM] + [ANY] * 8,
        out_specs=[VMEM] * (1 if 0 in order else 2),
        scratch_shapes=[
            pltpu.VMEM((4, D, D), BF),
            pltpu.VMEM((BD, K, BLK, BLK), BF),
            pltpu.VMEM(((BD + 2) * BLK, D), BF),
            pltpu.VMEM((BD * BLK, D), BF),
            pltpu.VMEM((n, D, D), BF),
            pltpu.VMEM((n, BLK, D), BF),
            pltpu.VMEM((n, BLK, D), BF),
            pltpu.SemaphoreType.DMA((4,)),
            pltpu.SemaphoreType.DMA,
            pltpu.SemaphoreType.DMA((n,)),
            pltpu.SemaphoreType.DMA((2, n)),
        ],
        compiler_params=params(20 if 0 in order else 60),
        cost_estimate=pl.CostEstimate(
            flops=2_000_000_000 * n, bytes_accessed=4_000_000, transcendentals=262144 * n
        ),
        name=f"first{n}",
    )(src, cnt, gain, inner, outer, samples, *ws, tiles)


def arrived_kernel(h0, near, far, mixed_a, mixed_b, out, sem):
    p = lax.axis_index("segment")

    @pl.when(p == 0)
    def _():
        pltpu.make_async_copy(h0, out, sem).start()

    for q in (1, 2, 3):

        @pl.when(p == q)
        def _():
            for j in range(4):
                which, at = layout(q, j)
                src = (near, far)[which]
                if q == 2:
                    src, at = (mixed_a, at) if which == 0 else (mixed_b, at - ROWS)
                pltpu.make_async_copy(
                    src.at[pl.ds(at, D)], out.at[:, pl.ds(j * BLK, BLK)], sem
                ).start()

    pltpu.make_async_copy(h0, out, sem).wait()


def arrived_call(*args):
    return pl.pallas_call(
        arrived_kernel,
        out_shape=jax.ShapeDtypeStruct((D, D), BF),
        in_specs=[ANY] * 5,
        out_specs=VMEM,
        scratch_shapes=[pltpu.SemaphoreType.DMA],
        compiler_params=params(4),
        name="arrived",
    )(*args)


def copies(kernel_name, plan, shapes, *args, mib=4, out=ANY):
    def kernel(*refs):
        ins, outs, sem = refs[: len(args)], refs[len(args) : -1], refs[-1]
        moves = [
            pltpu.make_async_copy(a, b, sem.at[i]) for i, (a, b) in enumerate(plan(ins, outs))
        ]
        for m in moves:
            m.start()
        for m in moves:
            m.wait()

    return pl.pallas_call(
        kernel,
        out_shape=[jax.ShapeDtypeStruct(shape, BF) for shape in shapes],
        in_specs=[ANY] * len(args),
        out_specs=[out] * len(shapes),
        scratch_shapes=[pltpu.SemaphoreType.DMA((4,))],
        compiler_params=params(mib),
        cost_estimate=pl.CostEstimate(flops=0, bytes_accessed=2_000_000, transcendentals=0),
        name=kernel_name,
    )(*args)


def edges(samples):
    def plan(ins, outs):
        core = place()[4]
        last = 3 * BLK
        return [
            (ins[0].at[:, pl.ds(pl.multiple_of((1 - core) * last, BLK), BLK)], outs[0]),
            (ins[0].at[:, pl.ds(pl.multiple_of(core * last, BLK), BLK)], outs[1]),
        ]

    return copies("edges", plan, [(4, BLK, D)] * 2, samples, mib=60, out=VMEM)


def joined(ring):
    def plan(ins, outs):
        return [(ins[r], outs[0].at[r]) for r in range(4)]

    return copies("joined", plan, [(4, D, HALF)], *ring)[0]


STAGE_BY_Y = {1: True, 2: True, 3: False}


def weights_kernel(section, *refs):
    own, stage = refs[:4], refs[4:6]
    out, sem = refs[-2:]
    p, dom, y, _, c = place()

    @pl.when(p == section)
    def _():
        for m in range(4):
            pltpu.make_async_copy(own[m].at[0, 0], out.at[m], sem.at[m]).start()

    @pl.when(p != section)
    def _():
        first = y if STAGE_BY_Y[section] else (dom >> 3) & 3
        for m in range(4):
            for core in range(2):
                cols = pl.multiple_of((c ^ core) * HALF, HALF)
                pltpu.make_async_copy(
                    stage[core].at[first ^ m], out.at[m, :, pl.ds(cols, HALF)], sem.at[m]
                ).start()

    for m in range(4):
        pltpu.make_async_copy(own[m].at[0, 0], out.at[m], sem.at[m]).wait()


def weights_call(section, own, stage):
    return pl.pallas_call(
        functools.partial(weights_kernel, section),
        out_shape=jax.ShapeDtypeStruct((4, D, D), BF),
        in_specs=[ANY] * 6,
        out_specs=VMEM,
        scratch_shapes=[pltpu.SemaphoreType.DMA((4,))],
        compiler_params=params(4),
        cost_estimate=pl.CostEstimate(flops=0, bytes_accessed=4_000_000, transcendentals=0),
        name=f"weights{section}",
    )(*own, *stage)


def tiles_kernel(section, own, near, far, mixed_a, mixed_b, tiles, codes, gain, meta, sem):
    for q in range(SEG):

        @pl.when(lax.axis_index("segment") == q)
        def _():
            x = q ^ section
            if x == 2:
                first, second, small = mixed_a, mixed_b, mixed_b.at[pl.ds(ROWS, META)]
            else:
                whole = {0: own, 1: near, 3: far}[x]
                first, second = whole, whole.at[pl.ds(ROWS, ROWS)]
                small = whole.at[pl.ds(2 * ROWS, META)]
            for i in range(2 * K):
                rows = pl.ds(i * BLK, BLK)
                pltpu.make_async_copy(first.at[rows], tiles.at[i], sem.at[0]).start()
                pltpu.make_async_copy(second.at[rows], tiles.at[2 * K + i], sem.at[1]).start()
            pltpu.make_async_copy(small, meta, sem.at[2]).start()

    pltpu.make_async_copy(own.at[pl.ds(2 * ROWS, META)], meta, sem.at[2]).wait()
    for half in range(2):
        there = tiles.at[pl.ds(half * 2 * K, 2 * K)]
        pltpu.make_async_copy(there, there, sem.at[half]).wait()
    m = meta[...].astype(F32)
    code = m[:8]
    codes[...] = jnp.where(code < 7.0, code, 0.0).astype(jnp.int32)
    gain[...] = jnp.concatenate(
        [m[1 + i : 2 + i] + (m[5 + i : 6 + i] + m[9 + i : 10 + i]) for i in range(4)], axis=1
    )
    for i in range(BD * K):
        used = jnp.broadcast_to(m[0:1, i : i + 1], (BLK, BLK)) < 7.0
        tiles[i] = jnp.where(used, tiles[i].astype(F32), 0.0).astype(BF)


def tiles_call(section, arrays):
    return pl.pallas_call(
        functools.partial(tiles_kernel, section),
        out_shape=[
            jax.ShapeDtypeStruct((BD * K, BLK, BLK), BF),
            jax.ShapeDtypeStruct((8, BLK), jnp.int32),
            jax.ShapeDtypeStruct((1, D), F32),
        ],
        in_specs=[ANY] * len(arrays),
        out_specs=[VMEM] * 3,
        scratch_shapes=[pltpu.VMEM((META, BLK), BF), pltpu.SemaphoreType.DMA((3,))],
        compiler_params=params(4),
        cost_estimate=pl.CostEstimate(flops=0, bytes_accessed=2_000_000, transcendentals=0),
        name=f"tiles{section}",
    )(*arrays)


def section_kernel(codes, gain, tiles, w, h, inner, outer, sender, out, sbuf, gbuf):
    sbuf[BLK : 5 * BLK, :] = sender[...]
    for at, block in zip(halo_places(), (inner, outer)):
        sbuf[pl.ds(at, BLK), :] = block[...]
    gather(lambda i: tiles[i], lambda i: codes[0, i], sbuf, gbuf)
    for i in range(2):
        rows = slice(i * HALF, (i + 1) * HALF)
        out[rows, :] = update_rows(h[rows, :], gbuf[rows, :], w, gain[...])


def section_call(section, codes, gain, tiles, w, h, inner, outer, sender):
    return pl.pallas_call(
        section_kernel,
        out_shape=jax.ShapeDtypeStruct((BD * BLK, D), BF),
        in_specs=[SMEM] + [VMEM] * 7,
        out_specs=VMEM,
        scratch_shapes=[
            pltpu.VMEM(((BD + 2) * BLK, D), BF),
            pltpu.VMEM((BD * BLK, D), BF),
        ],
        compiler_params=params(16),
        cost_estimate=pl.CostEstimate(
            flops=1_500_000_000, bytes_accessed=4_000_000, transcendentals=262144
        ),
        name=f"section{section}",
    )(codes, gain, tiles, w, h, inner, outer, sender)


def sender_kernel(h, w, full, inner, outer):
    core = place()[4]
    for i in range(2):
        rows = slice(i * HALF, (i + 1) * HALF)
        full[rows, :] = sender_rows(h[rows, :], w[0])
    inner[...] = full[pl.ds(pl.multiple_of((1 - core) * 3 * BLK, BLK), BLK), :]
    outer[...] = full[pl.ds(pl.multiple_of(core * 3 * BLK, BLK), BLK), :]


def sender_call(section, h, w):
    return pl.pallas_call(
        sender_kernel,
        out_shape=[
            jax.ShapeDtypeStruct((BD * BLK, D), BF),
            jax.ShapeDtypeStruct((BLK, D), BF),
            jax.ShapeDtypeStruct((BLK, D), BF),
        ],
        in_specs=[VMEM, VMEM],
        out_specs=[VMEM] * 3,
        compiler_params=params(8),
        cost_estimate=pl.CostEstimate(
            flops=270_000_000, bytes_accessed=1_500_000, transcendentals=262144
        ),
        name=f"sender{section}",
    )(h, w)


def after(values, *others):
    return lax.optimization_barrier((values, others))[0]


def over_segments(value, x):
    return lax.ppermute(value, "segment", by_segment(x))


def over_dom(value, pairs):
    return lax.ppermute(value, "dom", pairs)


def exchange(inner, outer):
    return over_dom(inner, OTHER_CORE), over_dom(outer, NEXT_CHIP)


def shards(samples, w_source, w_self, w_message, w_output, norm_gain, tile_source, tile_count, tile_value):
    p, dom, y, _, core = place()
    ws = [w_source, w_self, w_message, w_output]
    edge = edges(samples)
    inner, outer = exchange(*edge)

    m = jnp.where(p == 3, (dom >> 3) & 3, y)
    a, b, c, d = (lax.dynamic_slice(w[0, 0], (0, core * HALF), (D, HALF)) for w in ws)
    piece = jnp.where(m < 2, jnp.where(m == 0, a, b), jnp.where(m == 2, c, d))
    piece = after(piece, edge)
    x1, x3, x2 = over_segments(piece, 1), over_segments(piece, 3), over_segments(piece, 2)

    small = (tile_source, tile_count, norm_gain, inner, outer, samples, ws, tile_value)
    own, own_far = first_call((2, 1, 3), *small)
    near, far = over_segments(own, 1), over_segments(own_far, 3)
    (h0,) = first_call((0,), *small)
    mixed_b, mixed_a = over_segments(far[ROWS:], 1), over_segments(near[:ROWS], 3)
    arrays = [own, near, far, mixed_a, mixed_b]

    def ring(own, routes):
        return [own] + [over_dom(own, route) for route in routes]

    def both(pieces):
        return pieces, over_dom(pieces, OTHER_CORE)

    over_y = [by_y(x) for x in (1, 2, 3)]
    x1, x2, x3 = after((x1, x2, x3), own, own_far)
    ring1 = ring(jnp.where(p == 2, x3, jnp.where(p == 3, x2, x1)), over_y)
    then = jnp.where(p == 0, x2, jnp.where(p == 1, x3, x1))
    last = jnp.where(p == 0, x3, jnp.where(p == 1, x2, x1))
    ring2 = ring(after(then, ring1), over_y)
    last = after(last, ring1)
    ring3 = [last, over_dom(last, Z_EVEN), over_dom(last, Z_FAR), over_dom(last, Z_ODD)]
    stages, pieces2, pieces3 = {1: both(joined(ring1))}, joined(ring2), joined(ring3)
    h = arrived_call(h0, near, far, after(mixed_a, pieces2, pieces3), mixed_b)
    for section in range(1, SEG):
        w = weights_call(section, ws, stages[section])
        tiles, codes, gain = tiles_call(section, arrays)
        sender, inner, outer = sender_call(section, h, w)
        inner, outer = exchange(inner, outer)
        if section == 1:
            stages[2] = both(after(pieces2, inner, outer))
        elif section == 2:
            stages[3] = both(after(pieces3, inner, outer))
        h = section_call(section, codes, gain, tiles, w, h, inner, outer, sender)
    return h[None]


def solution(mesh):
    return jax.shard_map(
        shards,
        mesh=mesh,
        in_specs=(
            P(None, "dom", None),
            P("segment", None, None, None),
            P("segment", None, None, None),
            P("segment", None, None, None),
            P("segment", None, None, None),
            P("segment", None, None),
            P("segment", "dom", None),
            P("segment", "dom"),
            P("segment", "dom", None, None, None),
        ),
        out_specs=P("segment", "dom", None),
        check_vma=False,
    )
```

```python
import functools

import jax
import jax.numpy as jnp
from jax import lax
from jax.experimental import pallas as pl
from jax.experimental.pallas import tpu as pltpu
from jax.sharding import PartitionSpec as P

D = 512
BLK = 128
BD = 4
K = 6
SEG = 4
Y, Z = 4, 8
HALF = D // 2
META = 16
ROWS = 2 * K * BLK
BF = jnp.bfloat16
F32 = jnp.float32
ANY = pl.BlockSpec(memory_space=pl.ANY)
HBM = pl.BlockSpec(memory_space=pltpu.HBM)
SMEM = pl.BlockSpec(memory_space=pltpu.SMEM)
VMEM = pl.BlockSpec(memory_space=pltpu.VMEM)


def silu(v):
    return (0.5 * v) * (1.0 + jnp.tanh(0.5 * v))


def params(mib):
    return pltpu.CompilerParams(vmem_limit_bytes=mib * 2**20)


def by_segment(x):
    return [(i, i ^ x) for i in range(SEG)]


def dom_pairs(move):
    out = []
    for d in range(Z * Y * 2):
        z, y, c = move(d // (2 * Y), d // 2 % Y, d % 2)
        out.append((d, ((z % Z) * Y + y % Y) * 2 + c % 2))
    return out


def by_y(x):
    return dom_pairs(lambda z, y, c: (z, y ^ x, c))


Z_FAR = dom_pairs(lambda z, y, c: (z ^ 2, y, c))
Z_EVEN = dom_pairs(lambda z, y, c: (z ^ 1, y, c))
Z_ODD = dom_pairs(lambda z, y, c: (((z + 1) ^ 1) - 1, y, c))
OTHER_CORE = dom_pairs(lambda z, y, c: (z, y, c ^ 1))
NEXT_CHIP = [(d, (((d + 1) ^ 1) - 1) % (2 * Y * Z)) for d in range(2 * Y * Z)]


def place():
    p, dom = lax.axis_index("segment"), lax.axis_index("dom")
    return p, dom, (dom >> 1) & 3, (dom >> 3) & 1, dom & 1


def sender_rows(rows, w):
    return silu(jnp.dot(rows, w, preferred_element_type=F32)).astype(BF)


def halo_places():
    core = place()[4]
    return pl.multiple_of((1 - core) * (5 * BLK), BLK), pl.multiple_of(core * (5 * BLK), BLK)


def gather(tile, code, sbuf, gbuf):
    for b in range(BD):
        slots = range(b * K, (b + 1) * K)
        places = [pl.multiple_of(code(i) * BLK, BLK) for i in slots]
        got = jnp.dot(
            jnp.concatenate([tile(i) for i in slots], axis=1),
            jnp.concatenate([sbuf[pl.ds(at, BLK), :] for at in places], axis=0),
            preferred_element_type=F32,
        )
        gbuf[b * BLK : (b + 1) * BLK, :] = got.astype(BF)


def update_rows(h, gathered, w, gain):
    mixed = jnp.dot(h, w[1], preferred_element_type=F32)
    mixed = mixed + jnp.dot(gathered, w[2], preferred_element_type=F32)
    mean = jnp.mean(mixed * mixed, axis=-1, keepdims=True)
    update = silu(mixed * lax.rsqrt(mean + 1e-05) * gain).astype(BF)
    return (h.astype(F32) + jnp.dot(update, w[3], preferred_element_type=F32)).astype(BF)


def own_small(src, cnt, gain):
    dom = place()[1]
    row = lax.broadcasted_iota(jnp.int32, (META, BLK), 0)
    col = lax.broadcasted_iota(jnp.int32, (META, BLK), 1)
    meta = jnp.zeros((META, BLK), F32)
    for i in range(BD * K):
        used, code = own_slot(src, cnt, dom, i)
        meta = jnp.where((row == 0) & (col == i), jnp.where(used, code, 7).astype(F32), meta)
    left = gain[0]
    for part in range(3):
        piece = left.astype(BF).astype(F32)
        left = left - piece
        for i in range(4):
            meta = jnp.where(row == 1 + 4 * part + i, piece[:, i * BLK : (i + 1) * BLK], meta)
    return meta.astype(BF)


def own_slot(src, cnt, dom, i):
    b, k = divmod(i, K)
    return k < cnt[0, b], (src[0, b, k] - (dom * BD - 1) + 512) & 255


def first_kernel(order, src, cnt, gain, inner, outer, samples, w0, w1, w2, w3, tiles, *rest):
    outs, (wbuf, tbuf, sbuf, gbuf, hbuf, ibuf, obuf, wsem, tsem, hsem, esem) = rest[:-11], rest[-11:]
    p, dom, _, _, _ = place()

    @pl.when(p == 0)
    def _():
        for m, w in enumerate((w0, w1, w2, w3)):
            pltpu.make_async_copy(w.at[0, 0], wbuf.at[m], wsem.at[m]).start()
        for n, sample in enumerate(order):
            pltpu.make_async_copy(samples.at[sample], hbuf.at[n], hsem.at[n]).start()
            pltpu.make_async_copy(inner.at[sample], ibuf.at[n], esem.at[0, n]).start()
            pltpu.make_async_copy(outer.at[sample], obuf.at[n], esem.at[1, n]).start()
        pltpu.make_async_copy(tiles.at[0], tbuf, tsem).start()
        in_place = halo_places()

        def tile(i):
            b, k = divmod(i, K)
            used, _ = own_slot(src, cnt, dom, i)
            t = tbuf[b, k]
            return jnp.where(used, t, jnp.zeros_like(t))

        def code(i):
            used, at = own_slot(src, cnt, dom, i)
            return jnp.where(used, at, 0)

        for n, sample in enumerate(order):
            if n == 0:
                pltpu.make_async_copy(w0.at[0, 0], wbuf.at[0], wsem.at[0]).wait()
            pltpu.make_async_copy(samples.at[sample], hbuf.at[n], hsem.at[n]).wait()
            pltpu.make_async_copy(inner.at[sample], ibuf.at[n], esem.at[0, n]).wait()
            pltpu.make_async_copy(outer.at[sample], obuf.at[n], esem.at[1, n]).wait()
            for at, block in zip(in_place, (ibuf, obuf)):
                sbuf[pl.ds(at, BLK), :] = sender_rows(block[n], wbuf[0])
            for i in range(2):
                rows = slice(i * HALF, (i + 1) * HALF)
                sbuf[BLK + i * HALF : BLK + (i + 1) * HALF, :] = sender_rows(hbuf[n, rows, :], wbuf[0])
            if n == 0:
                pltpu.make_async_copy(tiles.at[0], tbuf, tsem).wait()
                for m, w in ((1, w1), (2, w2), (3, w3)):
                    pltpu.make_async_copy(w.at[0, 0], wbuf.at[m], wsem.at[m]).wait()
            gather(tile, code, sbuf, gbuf)
            for i in range(2):
                rows = slice(i * HALF, (i + 1) * HALF)
                new = update_rows(hbuf[n, rows, :], gbuf[rows, :], wbuf, gain[0])
                if sample == 0:
                    outs[0][rows, :] = new
                    continue
                for j in range(4):
                    which, at = layout(sample, j)
                    outs[which][at + i * HALF : at + (i + 1) * HALF, :] = new[:, j * BLK : (j + 1) * BLK]

    if 0 not in order:

        @pl.when(p != 0)
        def _():
            moves = [
                pltpu.make_async_copy(
                    tiles.at[0, b, k], out.at[pl.ds((b * K + k) * BLK, BLK)], wsem.at[n]
                )
                for n, out in enumerate(outs)
                for b in range(BD)
                for k in range(K)
            ]
            for m in moves:
                m.start()
            small = own_small(src, cnt, gain)
            for n, out in enumerate(outs):
                out[2 * ROWS :, :] = small
                there = out.at[pl.ds(0, 2 * ROWS)]
                pltpu.make_async_copy(there, there, wsem.at[n]).wait()


def layout(sample, j):
    if sample == 1:
        return 0, 2 * D + j * D
    if sample == 3:
        return 1, j * D
    return (0, j * D) if j < 2 else (1, 4 * D + (j - 2) * D)


def first_call(order, src, cnt, gain, inner, outer, samples, ws, tiles):
    n = len(order)
    shape = (D, D) if 0 in order else (2 * ROWS + META, BLK)
    return pl.pallas_call(
        functools.partial(first_kernel, order),
        out_shape=[jax.ShapeDtypeStruct(shape, BF)] * (1 if 0 in order else 2),
        in_specs=[SMEM, SMEM, VMEM] + [ANY] * 8,
        out_specs=[VMEM] * (1 if 0 in order else 2),
        scratch_shapes=[
            pltpu.VMEM((4, D, D), BF),
            pltpu.VMEM((BD, K, BLK, BLK), BF),
            pltpu.VMEM(((BD + 2) * BLK, D), BF),
            pltpu.VMEM((BD * BLK, D), BF),
            pltpu.VMEM((n, D, D), BF),
            pltpu.VMEM((n, BLK, D), BF),
            pltpu.VMEM((n, BLK, D), BF),
            pltpu.SemaphoreType.DMA((4,)),
            pltpu.SemaphoreType.DMA,
            pltpu.SemaphoreType.DMA((n,)),
            pltpu.SemaphoreType.DMA((2, n)),
        ],
        compiler_params=params(20 if 0 in order else 60),
        cost_estimate=pl.CostEstimate(
            flops=2_000_000_000 * n, bytes_accessed=4_000_000, transcendentals=262144 * n
        ),
        name=f"first{n}",
    )(src, cnt, gain, inner, outer, samples, *ws, tiles)


def arrived_kernel(h0, near, far, mixed_a, mixed_b, out, sem):
    p = lax.axis_index("segment")

    @pl.when(p == 0)
    def _():
        pltpu.make_async_copy(h0, out, sem).start()

    for q in (1, 2, 3):

        @pl.when(p == q)
        def _():
            for j in range(4):
                which, at = layout(q, j)
                src = (near, far)[which]
                if q == 2:
                    src, at = (mixed_a, at) if which == 0 else (mixed_b, at - ROWS)
                pltpu.make_async_copy(
                    src.at[pl.ds(at, D)], out.at[:, pl.ds(j * BLK, BLK)], sem
                ).start()

    pltpu.make_async_copy(h0, out, sem).wait()


def arrived_call(*args):
    return pl.pallas_call(
        arrived_kernel,
        out_shape=jax.ShapeDtypeStruct((D, D), BF),
        in_specs=[ANY] * 5,
        out_specs=VMEM,
        scratch_shapes=[pltpu.SemaphoreType.DMA],
        compiler_params=params(4),
        name="arrived",
    )(*args)


def copies(kernel_name, plan, shapes, *args):
    def kernel(*refs):
        ins, outs, sem = refs[: len(args)], refs[len(args) : -1], refs[-1]
        moves = [
            pltpu.make_async_copy(a, b, sem.at[i]) for i, (a, b) in enumerate(plan(ins, outs))
        ]
        for m in moves:
            m.start()
        for m in moves:
            m.wait()

    return pl.pallas_call(
        kernel,
        out_shape=[jax.ShapeDtypeStruct(shape, BF) for shape in shapes],
        in_specs=[ANY] * len(args),
        out_specs=[ANY] * len(shapes),
        scratch_shapes=[pltpu.SemaphoreType.DMA((12,))],
        compiler_params=params(4),
        cost_estimate=pl.CostEstimate(flops=0, bytes_accessed=2_000_000, transcendentals=0),
        name=kernel_name,
    )(*args)


def joined(ring):
    def plan(ins, outs):
        return [(ins[r], outs[0].at[r]) for r in range(4)]

    return copies("joined", plan, [(4, D, HALF)], *ring)[0]


STAGE_BY_Y = {1: True, 2: False, 3: True}


def weights_kernel(section, *refs):
    own, stage = refs[:4], refs[4:6]
    out, sem = refs[-2:]
    p, dom, y, _, c = place()

    @pl.when(p == section)
    def _():
        for m in range(4):
            pltpu.make_async_copy(own[m].at[0, 0], out.at[m], sem.at[m]).start()

    @pl.when(p != section)
    def _():
        first = y if STAGE_BY_Y[section] else (dom >> 3) & 3
        for m in range(4):
            for core in range(2):
                cols = pl.multiple_of((c ^ core) * HALF, HALF)
                pltpu.make_async_copy(
                    stage[core].at[first ^ m], out.at[m, :, pl.ds(cols, HALF)], sem.at[m]
                ).start()

    for m in range(4):
        pltpu.make_async_copy(own[m].at[0, 0], out.at[m], sem.at[m]).wait()


def weights_call(section, own, stage):
    return pl.pallas_call(
        functools.partial(weights_kernel, section),
        out_shape=jax.ShapeDtypeStruct((4, D, D), BF),
        in_specs=[ANY] * 6,
        out_specs=VMEM,
        scratch_shapes=[pltpu.SemaphoreType.DMA((4,))],
        compiler_params=params(4),
        cost_estimate=pl.CostEstimate(flops=0, bytes_accessed=4_000_000, transcendentals=0),
        name=f"weights{section}",
    )(*own, *stage)


def tiles_kernel(section, own, near, far, mixed_a, mixed_b, tiles, codes, gain, meta, sem):
    for q in range(SEG):

        @pl.when(lax.axis_index("segment") == q)
        def _():
            x = q ^ section
            if x == 2:
                first, second, small = mixed_a, mixed_b, mixed_b.at[pl.ds(ROWS, META)]
            else:
                whole = {0: own, 1: near, 3: far}[x]
                first, second = whole, whole.at[pl.ds(ROWS, ROWS)]
                small = whole.at[pl.ds(2 * ROWS, META)]
            for i in range(2 * K):
                rows = pl.ds(i * BLK, BLK)
                pltpu.make_async_copy(first.at[rows], tiles.at[i], sem.at[0]).start()
                pltpu.make_async_copy(second.at[rows], tiles.at[2 * K + i], sem.at[1]).start()
            pltpu.make_async_copy(small, meta, sem.at[2]).start()

    pltpu.make_async_copy(own.at[pl.ds(2 * ROWS, META)], meta, sem.at[2]).wait()
    for half in range(2):
        there = tiles.at[pl.ds(half * 2 * K, 2 * K)]
        pltpu.make_async_copy(there, there, sem.at[half]).wait()
    m = meta[...].astype(F32)
    code = m[:8]
    codes[...] = jnp.where(code < 7.0, code, 0.0).astype(jnp.int32)
    gain[...] = jnp.concatenate(
        [m[1 + i : 2 + i] + (m[5 + i : 6 + i] + m[9 + i : 10 + i]) for i in range(4)], axis=1
    )
    for i in range(BD * K):
        used = jnp.broadcast_to(m[0:1, i : i + 1], (BLK, BLK)) < 7.0
        tiles[i] = jnp.where(used, tiles[i].astype(F32), 0.0).astype(BF)


def tiles_call(section, arrays):
    return pl.pallas_call(
        functools.partial(tiles_kernel, section),
        out_shape=[
            jax.ShapeDtypeStruct((BD * K, BLK, BLK), BF),
            jax.ShapeDtypeStruct((8, BLK), jnp.int32),
            jax.ShapeDtypeStruct((1, D), F32),
        ],
        in_specs=[ANY] * len(arrays),
        out_specs=[VMEM] * 3,
        scratch_shapes=[pltpu.VMEM((META, BLK), BF), pltpu.SemaphoreType.DMA((3,))],
        compiler_params=params(4),
        cost_estimate=pl.CostEstimate(flops=0, bytes_accessed=2_000_000, transcendentals=0),
        name=f"tiles{section}",
    )(*arrays)


def section_kernel(codes, gain, tiles, w, h, inner, outer, sender, out, sbuf, gbuf):
    sbuf[BLK : 5 * BLK, :] = sender[...]
    for at, block in zip(halo_places(), (inner, outer)):
        sbuf[pl.ds(at, BLK), :] = block[...]
    gather(lambda i: tiles[i], lambda i: codes[0, i], sbuf, gbuf)
    for i in range(2):
        rows = slice(i * HALF, (i + 1) * HALF)
        out[rows, :] = update_rows(h[rows, :], gbuf[rows, :], w, gain[...])


def section_call(section, codes, gain, tiles, w, h, inner, outer, sender):
    return pl.pallas_call(
        section_kernel,
        out_shape=jax.ShapeDtypeStruct((BD * BLK, D), BF),
        in_specs=[SMEM] + [VMEM] * 7,
        out_specs=VMEM,
        scratch_shapes=[
            pltpu.VMEM(((BD + 2) * BLK, D), BF),
            pltpu.VMEM((BD * BLK, D), BF),
        ],
        compiler_params=params(16),
        cost_estimate=pl.CostEstimate(
            flops=1_500_000_000, bytes_accessed=4_000_000, transcendentals=262144
        ),
        name=f"section{section}",
    )(codes, gain, tiles, w, h, inner, outer, sender)


def sender_kernel(h, w, full, inner, outer):
    core = place()[4]
    for i in range(2):
        rows = slice(i * HALF, (i + 1) * HALF)
        full[rows, :] = sender_rows(h[rows, :], w[0])
    inner[...] = full[pl.ds(pl.multiple_of((1 - core) * 3 * BLK, BLK), BLK), :]
    outer[...] = full[pl.ds(pl.multiple_of(core * 3 * BLK, BLK), BLK), :]


def sender_call(section, h, w):
    return pl.pallas_call(
        sender_kernel,
        out_shape=[
            jax.ShapeDtypeStruct((BD * BLK, D), BF),
            jax.ShapeDtypeStruct((BLK, D), BF),
            jax.ShapeDtypeStruct((BLK, D), BF),
        ],
        in_specs=[VMEM, VMEM],
        out_specs=[VMEM] * 3,
        compiler_params=params(8),
        cost_estimate=pl.CostEstimate(
            flops=270_000_000, bytes_accessed=1_500_000, transcendentals=262144
        ),
        name=f"sender{section}",
    )(h, w)


def after(values, *others):
    return lax.optimization_barrier((values, others))[0]


def over_segments(value, x):
    return lax.ppermute(value, "segment", by_segment(x))


def over_dom(value, pairs):
    return lax.ppermute(value, "dom", pairs)


def exchange(inner, outer):
    return over_dom(inner, OTHER_CORE), over_dom(outer, NEXT_CHIP)


def shards(samples, w_source, w_self, w_message, w_output, norm_gain, tile_source, tile_count, tile_value):
    p, dom, y, _, core = place()
    ws = [w_source, w_self, w_message, w_output]
    edge = [samples[:, :BLK], samples[:, (BD - 1) * BLK :]]
    edge = [jnp.where(core == 0, edge[1], edge[0]), jnp.where(core == 0, edge[0], edge[1])]
    inner, outer = exchange(*edge)

    m = jnp.where(p == 2, (dom >> 3) & 3, y)
    a, b, c, d = (lax.dynamic_slice(w[0, 0], (0, core * HALF), (D, HALF)) for w in ws)
    piece = jnp.where(m < 2, jnp.where(m == 0, a, b), jnp.where(m == 2, c, d))
    piece = after(piece, edge)
    x1, x3, x2 = over_segments(piece, 1), over_segments(piece, 3), over_segments(piece, 2)

    small = (tile_source, tile_count, norm_gain, inner, outer, samples, ws, tile_value)
    own, own_far = first_call((2, 1, 3), *small)
    near, far = over_segments(own, 1), over_segments(own_far, 3)
    (h0,) = first_call((0,), *small)
    mixed_b, mixed_a = over_segments(far[ROWS:], 1), over_segments(near[:ROWS], 3)
    arrays = [own, near, far, mixed_a, mixed_b]

    def ring(own, routes, *waits):
        a, c = over_dom(own, routes[0]), over_dom(own, routes[2])
        b = over_dom(after(own, a, c, waits), routes[1])
        return [own, a, b, c]

    def both(pieces):
        return pieces, over_dom(pieces, OTHER_CORE)

    over_y, over_z = [by_y(x) for x in (1, 2, 3)], [Z_EVEN, Z_FAR, Z_ODD]
    x1, x2, x3 = after((x1, x2, x3), own, own_far)
    then = jnp.where(p == 2, x3, jnp.where(p == 3, x2, x1))
    ring1 = [then] + [over_dom(then, route) for route in over_y]
    then = jnp.where(p == 0, x2, jnp.where(p == 1, x3, x1))
    last = jnp.where(p == 0, x3, jnp.where(p == 1, x2, x1))
    stages = {1: both(joined(ring1))}
    then, last = after((then, last), near, far, stages[1])
    ring2, ring3 = [then] + [over_dom(then, route) for route in over_z], ring(last, over_y)
    stages[2] = both(joined(ring2))
    h = arrived_call(h0, near, far, mixed_a, mixed_b)
    for section in range(1, SEG):
        if section == 2:
            stages[3] = both(joined(after(ring3, h)))
        w = weights_call(section, ws, stages[section])
        tiles, codes, gain = tiles_call(section, arrays)
        sender, inner, outer = sender_call(section, h, w)
        inner, outer = exchange(inner, outer)
        h = section_call(section, codes, gain, tiles, w, h, inner, outer, sender)
    return h[None]


def solution(mesh):
    return jax.shard_map(
        shards,
        mesh=mesh,
        in_specs=(
            P(None, "dom", None),
            P("segment", None, None, None),
            P("segment", None, None, None),
            P("segment", None, None, None),
            P("segment", None, None, None),
            P("segment", None, None),
            P("segment", "dom", None),
            P("segment", "dom"),
            P("segment", "dom", None, None, None),
        ),
        out_specs=P("segment", "dom", None),
        check_vma=False,
    )
```

```python
import functools

import jax
import jax.numpy as jnp
from jax import lax
from jax.experimental import pallas as pl
from jax.experimental.pallas import tpu as pltpu
from jax.sharding import PartitionSpec as P

D = 512
BLK = 128
BD = 4
K = 6
SEG = 4
Y, Z = 4, 8
HALF = D // 2
META = 16
ROWS = 2 * K * BLK
BF = jnp.bfloat16
F32 = jnp.float32
ANY = pl.BlockSpec(memory_space=pl.ANY)
HBM = pl.BlockSpec(memory_space=pltpu.HBM)
SMEM = pl.BlockSpec(memory_space=pltpu.SMEM)
VMEM = pl.BlockSpec(memory_space=pltpu.VMEM)


def silu(v):
    return (0.5 * v) * (1.0 + jnp.tanh(0.5 * v))


def params(mib):
    return pltpu.CompilerParams(vmem_limit_bytes=mib * 2**20)


def by_segment(x):
    return [(i, i ^ x) for i in range(SEG)]


def dom_pairs(move):
    out = []
    for d in range(Z * Y * 2):
        z, y, c = move(d // (2 * Y), d // 2 % Y, d % 2)
        out.append((d, ((z % Z) * Y + y % Y) * 2 + c % 2))
    return out


def by_y(x):
    return dom_pairs(lambda z, y, c: (z, y ^ x, c))


Z_FAR = dom_pairs(lambda z, y, c: (z ^ 2, y, c))
Z_EVEN = dom_pairs(lambda z, y, c: (z ^ 1, y, c))
Z_ODD = dom_pairs(lambda z, y, c: (((z + 1) ^ 1) - 1, y, c))
OTHER_CORE = dom_pairs(lambda z, y, c: (z, y, c ^ 1))
NEXT_CHIP = [(d, (((d + 1) ^ 1) - 1) % (2 * Y * Z)) for d in range(2 * Y * Z)]


def place():
    p, dom = lax.axis_index("segment"), lax.axis_index("dom")
    return p, dom, (dom >> 1) & 3, (dom >> 3) & 1, dom & 1


def sender_rows(rows, w):
    return silu(jnp.dot(rows, w, preferred_element_type=F32)).astype(BF)


def halo_places():
    core = place()[4]
    return pl.multiple_of((1 - core) * (5 * BLK), BLK), pl.multiple_of(core * (5 * BLK), BLK)


def gather(tile, code, sbuf, gbuf):
    for b in range(BD):
        slots = range(b * K, (b + 1) * K)
        places = [pl.multiple_of(code(i) * BLK, BLK) for i in slots]
        got = jnp.dot(
            jnp.concatenate([tile(i) for i in slots], axis=1),
            jnp.concatenate([sbuf[pl.ds(at, BLK), :] for at in places], axis=0),
            preferred_element_type=F32,
        )
        gbuf[b * BLK : (b + 1) * BLK, :] = got.astype(BF)


def update_rows(h, gathered, w, gain):
    mixed = jnp.dot(h, w[1], preferred_element_type=F32)
    mixed = mixed + jnp.dot(gathered, w[2], preferred_element_type=F32)
    mean = jnp.mean(mixed * mixed, axis=-1, keepdims=True)
    update = silu(mixed * lax.rsqrt(mean + 1e-05) * gain).astype(BF)
    return (h.astype(F32) + jnp.dot(update, w[3], preferred_element_type=F32)).astype(BF)


def own_small(src, cnt, gain):
    dom = place()[1]
    row = lax.broadcasted_iota(jnp.int32, (META, BLK), 0)
    col = lax.broadcasted_iota(jnp.int32, (META, BLK), 1)
    meta = jnp.zeros((META, BLK), F32)
    for i in range(BD * K):
        used, code = own_slot(src, cnt, dom, i)
        meta = jnp.where((row == 0) & (col == i), jnp.where(used, code, 7).astype(F32), meta)
    left = gain[0]
    for part in range(3):
        piece = left.astype(BF).astype(F32)
        left = left - piece
        for i in range(4):
            meta = jnp.where(row == 1 + 4 * part + i, piece[:, i * BLK : (i + 1) * BLK], meta)
    return meta.astype(BF)


def own_slot(src, cnt, dom, i):
    b, k = divmod(i, K)
    return k < cnt[0, b], (src[0, b, k] - (dom * BD - 1) + 512) & 255


def first_kernel(order, src, cnt, gain, inner, outer, samples, w0, w1, w2, w3, tiles, *rest):
    outs, (wbuf, tbuf, sbuf, gbuf, hbuf, ibuf, obuf, wsem, tsem, hsem, esem) = rest[:-11], rest[-11:]
    p, dom, _, _, _ = place()

    @pl.when(p == 0)
    def _():
        for m, w in enumerate((w0, w1, w2, w3)):
            pltpu.make_async_copy(w.at[0, 0], wbuf.at[m], wsem.at[m]).start()
        for n, sample in enumerate(order):
            pltpu.make_async_copy(samples.at[sample], hbuf.at[n], hsem.at[n]).start()
            pltpu.make_async_copy(inner.at[sample], ibuf.at[n], esem.at[0, n]).start()
            pltpu.make_async_copy(outer.at[sample], obuf.at[n], esem.at[1, n]).start()
        pltpu.make_async_copy(tiles.at[0], tbuf, tsem).start()
        in_place = halo_places()

        def tile(i):
            b, k = divmod(i, K)
            used, _ = own_slot(src, cnt, dom, i)
            t = tbuf[b, k]
            return jnp.where(used, t, jnp.zeros_like(t))

        def code(i):
            used, at = own_slot(src, cnt, dom, i)
            return jnp.where(used, at, 0)

        for n, sample in enumerate(order):
            if n == 0:
                pltpu.make_async_copy(w0.at[0, 0], wbuf.at[0], wsem.at[0]).wait()
            pltpu.make_async_copy(samples.at[sample], hbuf.at[n], hsem.at[n]).wait()
            pltpu.make_async_copy(inner.at[sample], ibuf.at[n], esem.at[0, n]).wait()
            pltpu.make_async_copy(outer.at[sample], obuf.at[n], esem.at[1, n]).wait()
            for at, block in zip(in_place, (ibuf, obuf)):
                sbuf[pl.ds(at, BLK), :] = sender_rows(block[n], wbuf[0])
            for i in range(2):
                rows = slice(i * HALF, (i + 1) * HALF)
                sbuf[BLK + i * HALF : BLK + (i + 1) * HALF, :] = sender_rows(hbuf[n, rows, :], wbuf[0])
            if n == 0:
                pltpu.make_async_copy(tiles.at[0], tbuf, tsem).wait()
                for m, w in ((1, w1), (2, w2), (3, w3)):
                    pltpu.make_async_copy(w.at[0, 0], wbuf.at[m], wsem.at[m]).wait()
            gather(tile, code, sbuf, gbuf)
            for i in range(2):
                rows = slice(i * HALF, (i + 1) * HALF)
                new = update_rows(hbuf[n, rows, :], gbuf[rows, :], wbuf, gain[0])
                if sample == 0:
                    outs[0][rows, :] = new
                    continue
                for j in range(4):
                    which, at = layout(sample, j)
                    outs[which][at + i * HALF : at + (i + 1) * HALF, :] = new[:, j * BLK : (j + 1) * BLK]

    if 0 not in order:

        @pl.when(p != 0)
        def _():
            moves = [
                pltpu.make_async_copy(
                    tiles.at[0, b, k], out.at[pl.ds((b * K + k) * BLK, BLK)], wsem.at[n]
                )
                for n, out in enumerate(outs)
                for b in range(BD)
                for k in range(K)
            ]
            for m in moves:
                m.start()
            small = own_small(src, cnt, gain)
            for n, out in enumerate(outs):
                out[2 * ROWS :, :] = small
                there = out.at[pl.ds(0, 2 * ROWS)]
                pltpu.make_async_copy(there, there, wsem.at[n]).wait()


def layout(sample, j):
    if sample == 1:
        return 0, 2 * D + j * D
    if sample == 3:
        return 1, j * D
    return (0, j * D) if j < 2 else (1, 4 * D + (j - 2) * D)


def first_call(order, src, cnt, gain, inner, outer, samples, ws, tiles):
    n = len(order)
    shape = (D, D) if 0 in order else (2 * ROWS + META, BLK)
    return pl.pallas_call(
        functools.partial(first_kernel, order),
        out_shape=[jax.ShapeDtypeStruct(shape, BF)] * (1 if 0 in order else 2),
        in_specs=[SMEM, SMEM, VMEM] + [ANY] * 8,
        out_specs=[VMEM] * (1 if 0 in order else 2),
        scratch_shapes=[
            pltpu.VMEM((4, D, D), BF),
            pltpu.VMEM((BD, K, BLK, BLK), BF),
            pltpu.VMEM(((BD + 2) * BLK, D), BF),
            pltpu.VMEM((BD * BLK, D), BF),
            pltpu.VMEM((n, D, D), BF),
            pltpu.VMEM((n, BLK, D), BF),
            pltpu.VMEM((n, BLK, D), BF),
            pltpu.SemaphoreType.DMA((4,)),
            pltpu.SemaphoreType.DMA,
            pltpu.SemaphoreType.DMA((n,)),
            pltpu.SemaphoreType.DMA((2, n)),
        ],
        compiler_params=params(20 if 0 in order else 60),
        cost_estimate=pl.CostEstimate(
            flops=2_000_000_000 * n, bytes_accessed=4_000_000, transcendentals=262144 * n
        ),
        name=f"first{n}",
    )(src, cnt, gain, inner, outer, samples, *ws, tiles)


def arrived_kernel(h0, near, far, mixed_a, mixed_b, out, sem):
    p = lax.axis_index("segment")

    @pl.when(p == 0)
    def _():
        pltpu.make_async_copy(h0, out, sem).start()

    for q in (1, 2, 3):

        @pl.when(p == q)
        def _():
            for j in range(4):
                which, at = layout(q, j)
                src = (near, far)[which]
                if q == 2:
                    src, at = (mixed_a, at) if which == 0 else (mixed_b, at - ROWS)
                pltpu.make_async_copy(
                    src.at[pl.ds(at, D)], out.at[:, pl.ds(j * BLK, BLK)], sem
                ).start()

    pltpu.make_async_copy(h0, out, sem).wait()


def arrived_call(*args):
    return pl.pallas_call(
        arrived_kernel,
        out_shape=jax.ShapeDtypeStruct((D, D), BF),
        in_specs=[ANY] * 5,
        out_specs=VMEM,
        scratch_shapes=[pltpu.SemaphoreType.DMA],
        compiler_params=params(4),
        name="arrived",
    )(*args)


def copies(kernel_name, plan, shapes, *args):
    def kernel(*refs):
        ins, outs, sem = refs[: len(args)], refs[len(args) : -1], refs[-1]
        moves = [
            pltpu.make_async_copy(a, b, sem.at[i]) for i, (a, b) in enumerate(plan(ins, outs))
        ]
        for m in moves:
            m.start()
        for m in moves:
            m.wait()

    return pl.pallas_call(
        kernel,
        out_shape=[jax.ShapeDtypeStruct(shape, BF) for shape in shapes],
        in_specs=[ANY] * len(args),
        out_specs=[ANY] * len(shapes),
        scratch_shapes=[pltpu.SemaphoreType.DMA((12,))],
        compiler_params=params(4),
        cost_estimate=pl.CostEstimate(flops=0, bytes_accessed=2_000_000, transcendentals=0),
        name=kernel_name,
    )(*args)


def joined(ring):
    def plan(ins, outs):
        return [(ins[r], outs[0].at[r]) for r in range(4)]

    return copies("joined", plan, [(4, D, HALF)], *ring)[0]


STAGE_BY_Y = {1: True, 2: False, 3: True}


def weights_kernel(section, *refs):
    own, stage = refs[:4], refs[4:6]
    out, sem = refs[-2:]
    p, dom, y, _, c = place()

    @pl.when(p == section)
    def _():
        for m in range(4):
            pltpu.make_async_copy(own[m].at[0, 0], out.at[m], sem.at[m]).start()

    @pl.when(p != section)
    def _():
        first = y if STAGE_BY_Y[section] else (dom >> 3) & 3
        for m in range(4):
            for core in range(2):
                cols = pl.multiple_of((c ^ core) * HALF, HALF)
                pltpu.make_async_copy(
                    stage[core].at[first ^ m], out.at[m, :, pl.ds(cols, HALF)], sem.at[m]
                ).start()

    for m in range(4):
        pltpu.make_async_copy(own[m].at[0, 0], out.at[m], sem.at[m]).wait()


def weights_call(section, own, stage):
    return pl.pallas_call(
        functools.partial(weights_kernel, section),
        out_shape=jax.ShapeDtypeStruct((4, D, D), BF),
        in_specs=[ANY] * 6,
        out_specs=VMEM,
        scratch_shapes=[pltpu.SemaphoreType.DMA((4,))],
        compiler_params=params(4),
        cost_estimate=pl.CostEstimate(flops=0, bytes_accessed=4_000_000, transcendentals=0),
        name=f"weights{section}",
    )(*own, *stage)


def tiles_kernel(section, own, near, far, mixed_a, mixed_b, tiles, codes, gain, meta, sem):
    for q in range(SEG):

        @pl.when(lax.axis_index("segment") == q)
        def _():
            x = q ^ section
            if x == 2:
                first, second, small = mixed_a, mixed_b, mixed_b.at[pl.ds(ROWS, META)]
            else:
                whole = {0: own, 1: near, 3: far}[x]
                first, second = whole, whole.at[pl.ds(ROWS, ROWS)]
                small = whole.at[pl.ds(2 * ROWS, META)]
            for i in range(2 * K):
                rows = pl.ds(i * BLK, BLK)
                pltpu.make_async_copy(first.at[rows], tiles.at[i], sem.at[0]).start()
                pltpu.make_async_copy(second.at[rows], tiles.at[2 * K + i], sem.at[1]).start()
            pltpu.make_async_copy(small, meta, sem.at[2]).start()

    pltpu.make_async_copy(own.at[pl.ds(2 * ROWS, META)], meta, sem.at[2]).wait()
    for half in range(2):
        there = tiles.at[pl.ds(half * 2 * K, 2 * K)]
        pltpu.make_async_copy(there, there, sem.at[half]).wait()
    m = meta[...].astype(F32)
    code = m[:8]
    codes[...] = jnp.where(code < 7.0, code, 0.0).astype(jnp.int32)
    gain[...] = jnp.concatenate(
        [m[1 + i : 2 + i] + (m[5 + i : 6 + i] + m[9 + i : 10 + i]) for i in range(4)], axis=1
    )
    for i in range(BD * K):
        used = jnp.broadcast_to(m[0:1, i : i + 1], (BLK, BLK)) < 7.0
        tiles[i] = jnp.where(used, tiles[i].astype(F32), 0.0).astype(BF)


def tiles_call(section, arrays):
    return pl.pallas_call(
        functools.partial(tiles_kernel, section),
        out_shape=[
            jax.ShapeDtypeStruct((BD * K, BLK, BLK), BF),
            jax.ShapeDtypeStruct((8, BLK), jnp.int32),
            jax.ShapeDtypeStruct((1, D), F32),
        ],
        in_specs=[ANY] * len(arrays),
        out_specs=[VMEM] * 3,
        scratch_shapes=[pltpu.VMEM((META, BLK), BF), pltpu.SemaphoreType.DMA((3,))],
        compiler_params=params(4),
        cost_estimate=pl.CostEstimate(flops=0, bytes_accessed=2_000_000, transcendentals=0),
        name=f"tiles{section}",
    )(*arrays)


def section_kernel(codes, gain, tiles, w, h, inner, outer, sender, out, sbuf, gbuf):
    sbuf[BLK : 5 * BLK, :] = sender[...]
    for at, block in zip(halo_places(), (inner, outer)):
        sbuf[pl.ds(at, BLK), :] = block[...]
    gather(lambda i: tiles[i], lambda i: codes[0, i], sbuf, gbuf)
    for i in range(2):
        rows = slice(i * HALF, (i + 1) * HALF)
        out[rows, :] = update_rows(h[rows, :], gbuf[rows, :], w, gain[...])


def section_call(section, codes, gain, tiles, w, h, inner, outer, sender):
    return pl.pallas_call(
        section_kernel,
        out_shape=jax.ShapeDtypeStruct((BD * BLK, D), BF),
        in_specs=[SMEM] + [VMEM] * 7,
        out_specs=VMEM,
        scratch_shapes=[
            pltpu.VMEM(((BD + 2) * BLK, D), BF),
            pltpu.VMEM((BD * BLK, D), BF),
        ],
        compiler_params=params(16),
        cost_estimate=pl.CostEstimate(
            flops=1_500_000_000, bytes_accessed=4_000_000, transcendentals=262144
        ),
        name=f"section{section}",
    )(codes, gain, tiles, w, h, inner, outer, sender)


def sender_kernel(h, w, full, inner, outer):
    core = place()[4]
    for i in range(2):
        rows = slice(i * HALF, (i + 1) * HALF)
        full[rows, :] = sender_rows(h[rows, :], w[0])
    inner[...] = full[pl.ds(pl.multiple_of((1 - core) * 3 * BLK, BLK), BLK), :]
    outer[...] = full[pl.ds(pl.multiple_of(core * 3 * BLK, BLK), BLK), :]


def sender_call(section, h, w):
    return pl.pallas_call(
        sender_kernel,
        out_shape=[
            jax.ShapeDtypeStruct((BD * BLK, D), BF),
            jax.ShapeDtypeStruct((BLK, D), BF),
            jax.ShapeDtypeStruct((BLK, D), BF),
        ],
        in_specs=[VMEM, VMEM],
        out_specs=[VMEM] * 3,
        compiler_params=params(8),
        cost_estimate=pl.CostEstimate(
            flops=270_000_000, bytes_accessed=1_500_000, transcendentals=262144
        ),
        name=f"sender{section}",
    )(h, w)


def after(values, *others):
    return lax.optimization_barrier((values, others))[0]


def over_segments(value, x):
    return lax.ppermute(value, "segment", by_segment(x))


def over_dom(value, pairs):
    return lax.ppermute(value, "dom", pairs)


def exchange(inner, outer):
    return over_dom(inner, OTHER_CORE), over_dom(outer, NEXT_CHIP)


def shards(samples, w_source, w_self, w_message, w_output, norm_gain, tile_source, tile_count, tile_value):
    p, dom, y, _, core = place()
    ws = [w_source, w_self, w_message, w_output]
    edge = [samples[:, :BLK], samples[:, (BD - 1) * BLK :]]
    edge = [jnp.where(core == 0, edge[1], edge[0]), jnp.where(core == 0, edge[0], edge[1])]
    inner, outer = exchange(*edge)

    m = jnp.where(p == 2, (dom >> 3) & 3, y)
    a, b, c, d = (lax.dynamic_slice(w[0, 0], (0, core * HALF), (D, HALF)) for w in ws)
    piece = jnp.where(m < 2, jnp.where(m == 0, a, b), jnp.where(m == 2, c, d))
    piece = after(piece, edge)
    x1, x3, x2 = over_segments(piece, 1), over_segments(piece, 3), over_segments(piece, 2)

    small = (tile_source, tile_count, norm_gain, inner, outer, samples, ws, tile_value)
    own, own_far = first_call((2, 1, 3), *small)
    near, far = over_segments(own, 1), over_segments(own_far, 3)
    (h0,) = first_call((0,), *small)
    mixed_b, mixed_a = over_segments(far[ROWS:], 1), over_segments(near[:ROWS], 3)
    arrays = [own, near, far, mixed_a, mixed_b]

    def ring(own, routes, *waits):
        a, c = over_dom(own, routes[0]), over_dom(own, routes[2])
        b = over_dom(after(own, a, c, waits), routes[1])
        return [own, a, b, c]

    def both(pieces):
        return pieces, over_dom(pieces, OTHER_CORE)

    over_y, over_z = [by_y(x) for x in (1, 2, 3)], [Z_EVEN, Z_FAR, Z_ODD]
    x1, x2, x3 = after((x1, x2, x3), own, own_far)
    then = jnp.where(p == 2, x3, jnp.where(p == 3, x2, x1))
    ring1 = [then] + [over_dom(then, route) for route in over_y]
    then = jnp.where(p == 0, x2, jnp.where(p == 1, x3, x1))
    last = jnp.where(p == 0, x3, jnp.where(p == 1, x2, x1))
    stages = {1: both(joined(ring1))}
    then, last = after((then, last), near, far, stages[1])
    ring2, ring3 = [then] + [over_dom(then, route) for route in over_z], ring(last, over_y)
    h = arrived_call(h0, near, far, mixed_a, mixed_b)
    for section in range(1, SEG):
        if section == 2:
            stages[3] = both(joined(after(ring3, h)))
        w = weights_call(section, ws, stages[section])
        tiles, codes, gain = tiles_call(section, arrays)
        sender, inner, outer = sender_call(section, h, w)
        if section == 1:
            stages[2] = both(joined(after(ring2, sender)))
        inner, outer = exchange(inner, outer)
        h = section_call(section, codes, gain, tiles, w, h, inner, outer, sender)
    return h[None]


def solution(mesh):
    return jax.shard_map(
        shards,
        mesh=mesh,
        in_specs=(
            P(None, "dom", None),
            P("segment", None, None, None),
            P("segment", None, None, None),
            P("segment", None, None, None),
            P("segment", None, None, None),
            P("segment", None, None),
            P("segment", "dom", None),
            P("segment", "dom"),
            P("segment", "dom", None, None, None),
        ),
        out_specs=P("segment", "dom", None),
        check_vma=False,
    )
```
